32 devices in a mesh: expert: 16 (over z, y, x), hidden: 2 (over core).
Axes of the slice: x: 2, y: 2, z: 4, core: 2. Of those that a mesh axis runs over, the one named last changes fastest.
Arguments:
- tokens: bfloat16 [1024, 4096], P('expert', 'hidden'), may hold values from -6 to 6
- expert_ids: int32 [1024, 8], P('expert'), may hold values from 0 to 15, all different within a row; in each aligned block of 64 rows (0 to 63, 64 to 127, ...) at most 64 rows name the same one
- gate_weights: float32 [1024, 8], P('expert'), may hold values from 0.05 to 0.5
- gate_proj: bfloat16 [16, 1536, 4096], P('expert', 'hidden'), may hold values from -0.09375 to 0.09375
- up_proj: bfloat16 [16, 1536, 4096], P('expert', 'hidden'), may hold values from -0.09375 to 0.09375
- down_proj: bfloat16 [16, 1536, 4096], P('expert', None, 'hidden'), may hold values from -0.15625 to 0.15625
Outputs:
- moe_out: bfloat16 [1024, 4096], P('expert', 'hidden')
The draws below stay inside these ranges and needn't reach their ends.
Inputs may be any that keep to these rules, and one draw needn't show every extreme that they name: `expert_ids`: each row names 8 different experts; in each aligned block of 64 rows no expert is named by more than 64 rows.
All inputs are finite; a program needn't handle non-finite values.
Results may differ from the reference program's by a relative error of at most 0.0057.
Values may be sent and summed in bfloat16 or wider, within the bound.
A program may use at most 64 MiB of HBM per device.

```python
import math
import jax
import jax.numpy as jnp
import numpy as np
from jax import lax

D = 4096
FF = 1536
TOP = 8
TOK_DEV = 64
EXPERTS = 16
TOKENS = 1024
CAP = 64
N_EXPERT = 16


def block_scale(rng, extent, shards, low, high):
    gain, own = 1.0, jax.random.fold_in(rng, 6)
    for dim, parts in shards:
        draws = jnp.exp(jax.random.uniform(jax.random.fold_in(own, dim), (parts,), jnp.float32, low / len(shards), high / len(shards)))
        gain = gain * jnp.repeat(draws, extent[dim] // parts).reshape([-1 if axis == dim else 1 for axis in range(len(extent))])
    return gain


def deal_out(key, own, number, rows, count, top, bound, lean):
    ranking = jax.random.permutation(key, count)
    heavy_load, ordinary = portions_of(count, rows * top, bound, lean, True), portions_of(count, rows * top, bound, lean, False)
    places = jnp.arange(count)

    def named(sizes, rotation):
        used = int((sizes > 0).sum())
        fixed = max(1, used // 4)
        passed = fixed + (places - fixed + rotation * (used - fixed)) % max(1, count - fixed)
        return jnp.zeros((count,), jnp.int32).at[ranking[jnp.where(places < fixed, places, passed)]].set(jnp.asarray(sizes, jnp.int32))

    sizes = jnp.where(number % 4 == 0, named(heavy_load, number // 4), named(ordinary, number - number // 4 - 1))
    mixed = jax.random.permutation(jax.random.fold_in(own, 3), count)
    giver, sink = mixed[0:count // 2 * 2:2], mixed[1:count // 2 * 2:2]
    margin = jnp.minimum(sizes[giver] - 1, bound - sizes[sink]) // 2
    margin = jnp.where((giver == ranking[0]) | (sink == ranking[0]) | (sizes[sink] == 0), 0, jnp.maximum(margin, 0))
    passed = jax.random.randint(jax.random.fold_in(own, 4), (count // 2,), 0, 1 << 20) % (margin + 1)
    sizes = sizes.at[giver].add(-passed).at[sink].add(passed)
    labels = jnp.searchsorted(jnp.cumsum(sizes), jnp.arange(rows * top), side="right").astype(jnp.int32)
    listing = labels.reshape(top, rows).T
    listing = listing[jax.random.permutation(jax.random.fold_in(own, 1), rows)]
    rotation = jax.random.randint(jax.random.fold_in(own, 2), (rows, 1), 0, top)
    return jnp.take_along_axis(listing, (jnp.arange(top)[None, :] + rotation) % top, axis=1)


def portions_of(count, total, most, slope, full):
    weights = [(1 << 20) // math.isqrt(standing ** slope) + 1 for standing in range(1, count + 1)]
    largest = most if full else min(most, max(-(-total // count), total * weights[0] // sum(weights)))
    least = 1 if total - largest >= count - 1 else 0
    given, surplus = [largest] + [least] * (count - 1), total - largest - least * (count - 1)
    while surplus > 0:
        free = [i for i in range(1, count) if given[i] < largest] or [i for i in range(1, count) if given[i] < most]
        pool, remaining = sum([weights[i] for i in free]), surplus
        for i in free:
            addition = min(most - given[i], max(1, remaining * weights[i] // pool), surplus)
            given[i] = given[i] + addition
            surplus = surplus - addition
    return np.array(given)


def centred(rng, dims, scale, bound, pieces=(), held_as=jnp.bfloat16):
    drawn = jax.random.normal(rng, dims, jnp.float32) * scale
    if len(pieces) > 0:
        drawn = block_scale(rng, dims, pieces, -0.22, 0.18) * drawn
    return jnp.clip(drawn, min=-bound, max=bound).astype(held_as)


def setup_inputs(seed: int = 0) -> dict:
    arg_keys = jax.random.split(jax.random.key(seed), 7)
    tokens = centred(arg_keys[0], (TOKENS, D), 1.0, 6.0, ((0, 16), (1, 2)))
    expert_ids_keys = jax.random.split(jax.random.fold_in(arg_keys[1], 1), TOKENS // TOK_DEV)
    expert_ids_turns = jax.random.permutation(jax.random.fold_in(arg_keys[1], 3), TOKENS // TOK_DEV)
    expert_ids = jax.vmap(lambda own, number: deal_out(jax.random.fold_in(arg_keys[1], 2), own, number, TOK_DEV, EXPERTS, TOP, CAP, 2))(expert_ids_keys, expert_ids_turns).reshape((TOKENS, TOP))
    gate_weights = jnp.clip(jnp.exp(math.log(0.5) - 2.3025851 * jax.random.uniform(arg_keys[2], (TOKENS, TOP), jnp.float32) ** block_scale(arg_keys[2], (TOKENS, TOP), ((0, 16),), -0.2, 0.2)), 0.05, 0.5)
    gate_proj = centred(arg_keys[3], (EXPERTS, FF, D), D ** -0.5, 0.09375, ((0, 16), (1, 2)))
    up_proj = centred(arg_keys[4], (EXPERTS, FF, D), D ** -0.5, 0.09375, ((0, 16), (1, 2)))
    down_proj = centred(arg_keys[5], (EXPERTS, FF, D), FF ** -0.5, 0.15625, ((0, 16), (2, 2)))
    return {"tokens": tokens, "expert_ids": expert_ids, "gate_weights": gate_weights, "gate_proj": gate_proj, "up_proj": up_proj, "down_proj": down_proj}


def reference(tokens, expert_ids, gate_weights, gate_proj, up_proj, down_proj):
    flat_ids = expert_ids.reshape(-1).astype(jnp.int32)
    onehot = (flat_ids[:, None] == jnp.arange(EXPERTS, dtype=jnp.int32)[None, :]).astype(jnp.int32)
    blocks = onehot.reshape(N_EXPERT, TOK_DEV * TOP, EXPERTS)
    ranks = jnp.cumsum(blocks, axis=1) - blocks
    slot_index = jnp.sum(ranks * blocks, axis=2).reshape(-1).astype(jnp.int32)
    pair_index = jnp.arange(TOKENS * TOP, dtype=jnp.int32)
    source_block = pair_index // (TOK_DEV * TOP)
    position = (source_block * CAP + slot_index).astype(jnp.int32)
    token_index = (pair_index // TOP).astype(jnp.int32)
    row_token = jnp.zeros((EXPERTS, N_EXPERT * CAP), jnp.int32).at[flat_ids, position].set(token_index)
    row_gate = jnp.zeros((EXPERTS, N_EXPERT * CAP), gate_weights.dtype).at[flat_ids, position].set(gate_weights.reshape(-1))

    def expert_step(running, inputs):
        w_gate, w_up, w_down, rows_idx, rows_gate = inputs
        picked = tokens[rows_idx]
        gate_sum = jnp.dot(picked, w_gate.T, preferred_element_type=jnp.float32)
        up_sum = jnp.dot(picked, w_up.T, preferred_element_type=jnp.float32)
        activation = (jax.nn.silu(gate_sum) * up_sum).astype(jnp.bfloat16)
        expert_out = jnp.dot(activation, w_down, preferred_element_type=jnp.float32).astype(jnp.bfloat16)
        weighted = rows_gate[:, None] * expert_out.astype(jnp.float32)
        return running.at[rows_idx].add(weighted), None

    start_sum = jnp.zeros((TOKENS, D), jnp.float32)
    mixed, _ = lax.scan(expert_step, start_sum, (gate_proj, up_proj, down_proj, row_token, row_gate))
    return mixed.astype(jnp.bfloat16)
```

```python
import functools

import jax
import jax.numpy as jnp
from jax import lax
from jax.experimental import pallas as pl
from jax.experimental.pallas import tpu as pltpu
from jax.sharding import PartitionSpec as P

MESH = pl.DeviceIdType.MESH
NZ, NY, NX = 4, 2, 2
ROWS = 16
TILE = 256


def routed(tokens, expert_ids, gate_weights, gate_proj, up_proj, down_proj):
    local_count = gate_proj.shape[0]
    experts_all = local_count * lax.axis_size("expert")
    tok_rows = tokens.shape[0]
    top_count = expert_ids.shape[1]
    capacity = 2 * tok_rows * top_count // experts_all
    flat_ids = expert_ids.reshape(-1)
    onehot = (flat_ids[:, None] == jnp.arange(experts_all, dtype=jnp.int32)[None, :]).astype(
        jnp.int32
    )
    slot_index = jnp.sum((jnp.cumsum(onehot, axis=0) - onehot) * onehot, axis=1)
    position = flat_ids * capacity + slot_index
    token_of = jnp.arange(tok_rows * top_count, dtype=jnp.int32) // top_count
    full_rows = lax.all_gather(tokens, "hidden", axis=1, tiled=True)
    packed = jnp.zeros((experts_all * capacity, full_rows.shape[1]), full_rows.dtype)
    packed = packed.at[position].set(full_rows[token_of])
    arrived = lax.all_to_all(
        packed.reshape(experts_all, capacity, full_rows.shape[1]),
        "expert",
        split_axis=0,
        concat_axis=1,
        tiled=True,
    )
    gate_sum = jnp.einsum("lrd,lfd->lfr", arrived, gate_proj, preferred_element_type=jnp.float32)
    up_sum = jnp.einsum("lrd,lfd->lfr", arrived, up_proj, preferred_element_type=jnp.float32)
    activation = (jax.nn.silu(gate_sum) * up_sum).astype(jnp.bfloat16)
    expert_out = jnp.einsum(
        "lfr,lfd->lrd",
        lax.all_gather(activation, "hidden", axis=1, tiled=True),
        down_proj,
        preferred_element_type=jnp.float32,
    ).astype(jnp.bfloat16)
    returned = lax.all_to_all(expert_out, "expert", split_axis=1, concat_axis=0, tiled=True)
    gathered = returned.reshape(experts_all * capacity, returned.shape[2])[position]
    gathered = gathered.reshape(tok_rows, top_count, returned.shape[2]).astype(jnp.float32)
    mixed = jnp.sum(gathered * gate_weights[:, :, None], axis=1)
    return mixed.astype(jnp.bfloat16)


def dense_kernel(
    tok_ref, wmat_ref, gate_hbm, up_hbm, down_hbm, out_ref,
    x_buf, w_buf, w_col, gate, up, down, act, part, red1, red2, red3,
    local_sem, send_sem, recv_sem,
):
    chunks = tok_ref.shape[0] // ROWS
    wide = x_buf.shape[-1]
    rows = NZ * NY * NX * ROWS
    hid = gate.shape[0]
    f32, bf16 = jnp.float32, jnp.bfloat16
    me = lax.axis_index("expert")
    core = lax.axis_index("hidden")
    z, y, x = me // (NY * NX), (me // NX) % NY, me % NX

    def at(zz, yy, xx):
        return ((zz * NY + yy) * NX + xx, core)

    x_peer, y_peer, sibling = at(z, y, 1 - x), at(z, 1 - y, x), (me, 1 - core)
    z_of = [lax.rem(z + d, NZ) for d in range(NZ)]
    z_peers = [at(z_of[d], y, x) for d in range(NZ)]

    loads = [
        pltpu.make_async_copy(src, dst, local_sem.at[i])
        for i, (src, dst) in enumerate(((gate_hbm, gate), (up_hbm, up), (down_hbm, down)))
    ]
    for load in loads:
        load.start()

    barrier = pltpu.get_barrier_semaphore()
    peers = [x_peer, y_peer, sibling] + z_peers[1:]
    for peer in peers:
        pl.semaphore_signal(barrier, inc=1, device_id=peer, device_id_type=MESH)
    for c in range(chunks):
        for p in range(2):
            x_buf[(c * 2 + core) * 2 + p, z, y, x] = tok_ref[
                c * ROWS : (c + 1) * ROWS, p * wide : (p + 1) * wide
            ]
    w_buf[z, y, x] = wmat_ref[...]
    pl.semaphore_wait(barrier, len(peers))

    sent = []

    def send(src, dst, peer):
        k = len(sent)
        copy = pltpu.make_async_remote_copy(
            src_ref=src, dst_ref=dst, send_sem=send_sem.at[k], recv_sem=recv_sem.at[k],
            device_id=peer, device_id_type=MESH,
        )
        copy.start()
        sent.append(copy)
        return copy

    def arrive(copies):
        for copy in copies:
            copy.wait_recv()

    def move(ref, peer):
        return send(ref, ref, peer)

    def spread_z(c):
        own = x_buf.at[pl.ds((c * 2 + core) * 2, 2), z, y, x]
        return [move(own, z_peers[d]) for d in range(1, NZ)]

    def spread_1(c):
        i = (c * 2 + core) * 2
        return [move(x_buf.at[i, :, y, x], x_peer), move(x_buf.at[i + 1, :, y, x], y_peer)]

    def spread_2(c):
        i = (c * 2 + core) * 2
        return [move(x_buf.at[i, :, y], y_peer), move(x_buf.at[i + 1, :, :, x], x_peer)]

    def spread_core(c):
        return [move(x_buf.at[pl.ds((c * 2 + core) * 2, 2)], sibling)]

    def gate_up(c):
        def step(n, carry):
            cols = pl.ds(pl.multiple_of(n * TILE, TILE), TILE)
            sums = []
            for weight in (gate, up):
                total = None
                for k in range(4):
                    term = lax.dot_general(
                        x_buf[c * 4 + k].reshape(rows, wide),
                        weight[cols, k * wide : (k + 1) * wide],
                        (((1,), (1,)), ((), ())),
                        preferred_element_type=f32,
                    )
                    total = term if total is None else total + term
                sums.append(total)
            g, u = sums
            act[c * 2 + core, :, cols] = ((g / (1.0 + jnp.exp(-g))) * u).astype(bf16)
            return carry

        lax.fori_loop(0, hid // TILE, step, 0)
        return [move(act.at[c * 2 + core], sibling)]

    def down_part(c, p):
        def step(n, carry):
            into = pl.ds(pl.multiple_of(n * TILE, TILE), TILE)
            cols = pl.ds(pl.multiple_of(p * wide + n * TILE, TILE), TILE)
            total = None
            for k in range(2):
                term = jnp.dot(
                    act[c * 2 + k], down[k * hid : (k + 1) * hid, cols],
                    preferred_element_type=f32,
                )
                total = term if total is None else total + term
            scale = w_col[c]
            total = total * jnp.concatenate([scale, scale], axis=1)
            part[c * 2 + p, :, :, :, :, into] = total.astype(bf16).reshape(
                NZ, NY, NX, ROWS, TILE
            )
            return carry

        lax.fori_loop(0, wide // TILE, step, 0)

    def down_all(c):
        down_part(c, 0)
        first = send(part.at[c * 2, :, 1 - y], red1.at[c * 2], y_peer)
        down_part(c, 1)
        return [first, send(part.at[c * 2 + 1, :, :, 1 - x], red1.at[c * 2 + 1], x_peer)]

    def reduce_1(c, copies):
        copies[0].wait_recv()
        for zz in range(NZ):
            red1[c * 2, zz] = (
                red1[c * 2, zz].astype(f32) + part[c * 2, zz, y].astype(f32)
            ).astype(bf16)
        first = send(red1.at[c * 2, :, 1 - x], red2.at[c * 2], x_peer)
        copies[1].wait_recv()
        for zz in range(NZ):
            for yy in range(NY):
                red1[c * 2 + 1, zz, yy] = (
                    red1[c * 2 + 1, zz, yy].astype(f32) + part[c * 2 + 1, zz, yy, x].astype(f32)
                ).astype(bf16)
        return [first, send(red1.at[c * 2 + 1, :, 1 - y], red2.at[c * 2 + 1], y_peer)]

    def reduce_2(c, copies):
        for p, (copy, mine) in enumerate(zip(copies, (x, y))):
            copy.wait_recv()
            for zz in range(NZ):
                red2[c * 2 + p, zz] = (
                    red2[c * 2 + p, zz].astype(f32) + red1[c * 2 + p, zz, mine].astype(f32)
                ).astype(bf16)
        return [
            send(red2.at[pl.ds(c * 2, 2), z_of[d]], red3.at[c, d - 1], z_peers[d])
            for d in range(1, NZ)
        ]

    def finish(c, copies):
        arrive(copies)
        for p in range(2):
            total = red2[c * 2 + p, z].astype(f32)
            for d in range(NZ - 1):
                total = total + red3[c, d, p].astype(f32)
            out_ref[c * ROWS : (c + 1) * ROWS, p * wide : (p + 1) * wide] = total.astype(bf16)

    def columns_of_weights():
        lane = lax.broadcasted_iota(jnp.int32, w_buf.shape[3:], 0)
        picked = [
            jnp.sum(jnp.where(lane == me, w_buf[zz, yy, xx], 0.0), axis=0, keepdims=True)
            for zz in range(NZ) for yy in range(NY) for xx in range(NX)
        ]
        square = jnp.concatenate(picked + [jnp.zeros((128 - len(picked), 128), f32)], axis=0)
        turned = square.T
        for c in range(chunks):
            for b in range(len(picked)):
                w_col[c, b * ROWS : (b + 1) * ROWS, :] = jnp.broadcast_to(
                    turned[c * ROWS : (c + 1) * ROWS, b : b + 1], (ROWS, 128)
                )

    za = [None] * chunks
    s1, s2, sc = [None] * chunks, [None] * chunks, [None] * chunks
    aa, r1, r2, r3 = [None] * chunks, [None] * chunks, [None] * chunks, [None] * chunks

    za[0] = spread_z(0)
    wz = [move(w_buf.at[z, y, x], z_peers[d]) for d in range(1, NZ)]
    za[1] = spread_z(1)
    arrive(za[0])
    s1[0] = spread_1(0)
    arrive(wz)
    wx = [move(w_buf.at[:, y, x], x_peer)]
    za[2] = spread_z(2)
    arrive(s1[0])
    s2[0] = spread_2(0)
    arrive(wx)
    wy = [move(w_buf.at[:, y], y_peer)]
    arrive(za[1])
    s1[1] = spread_1(1)
    za[3] = spread_z(3)
    arrive(s1[1])
    s2[1] = spread_2(1)
    arrive(wy)
    columns_of_weights()
    arrive(s2[0])
    sc[0] = spread_core(0)
    arrive(za[2])
    s1[2] = spread_1(2)
    loads[0].wait()
    loads[1].wait()
    loads[2].wait()
    arrive(sc[0])
    aa[0] = gate_up(0)
    arrive(s1[2])
    s2[2] = spread_2(2)
    arrive(s2[1])
    sc[1] = spread_core(1)
    arrive(za[3])
    s1[3] = spread_1(3)
    arrive(sc[1])
    aa[1] = gate_up(1)
    arrive(s1[3])
    s2[3] = spread_2(3)
    arrive(aa[0])
    r1[0] = down_all(0)
    arrive(s2[2])
    sc[2] = spread_core(2)
    arrive(aa[1])
    r1[1] = down_all(1)
    arrive(sc[2])
    aa[2] = gate_up(2)
    r2[0] = reduce_1(0, r1[0])
    arrive(s2[3])
    sc[3] = spread_core(3)
    arrive(aa[2])
    r1[2] = down_all(2)
    arrive(sc[3])
    aa[3] = gate_up(3)
    r2[1] = reduce_1(1, r1[1])
    r3[0] = reduce_2(0, r2[0])
    arrive(aa[3])
    r1[3] = down_all(3)
    r2[2] = reduce_1(2, r1[2])
    r3[1] = reduce_2(1, r2[1])
    finish(0, r3[0])
    r2[3] = reduce_1(3, r1[3])
    r3[2] = reduce_2(2, r2[2])
    finish(1, r3[1])
    r3[3] = reduce_2(3, r2[3])
    finish(2, r3[2])
    finish(3, r3[3])
    for copy in sent:
        copy.wait_send()


def dense(tokens, expert_ids, gate_weights, gate_proj, up_proj, down_proj):
    tok_rows, half = tokens.shape
    experts_all = lax.axis_size("expert")
    hid, width = gate_proj.shape[1:]
    chunks = tok_rows // ROWS
    wide = half // 2
    rows = experts_all * ROWS
    chosen = expert_ids[None, :, :] == jnp.arange(experts_all, dtype=jnp.int32)[:, None, None]
    wmat = jnp.sum(jnp.where(chosen, gate_weights[None], 0.0), axis=2)
    wmat = jnp.pad(wmat, ((0, 0), (0, 128 - tok_rows)))
    bf16, f32 = jnp.bfloat16, jnp.float32
    vmem = pl.BlockSpec(memory_space=pltpu.VMEM)
    hbm = pl.BlockSpec(memory_space=pl.ANY)
    copies = chunks * 16 + 5
    return pl.pallas_call(
        dense_kernel,
        out_shape=jax.ShapeDtypeStruct((tok_rows, half), bf16),
        in_specs=[vmem, vmem, hbm, hbm, hbm],
        out_specs=vmem,
        scratch_shapes=[
            pltpu.VMEM((chunks * 4, NZ, NY, NX, ROWS, wide), bf16),
            pltpu.VMEM((NZ, NY, NX, experts_all, 128), f32),
            pltpu.VMEM((chunks, rows, 128), f32),
            pltpu.VMEM((hid, width), bf16),
            pltpu.VMEM((hid, width), bf16),
            pltpu.VMEM((2 * hid, half), bf16),
            pltpu.VMEM((chunks * 2, rows, hid), bf16),
            pltpu.VMEM((chunks * 2, NZ, NY, NX, ROWS, wide), bf16),
            pltpu.VMEM((chunks * 2, NZ, 2, ROWS, wide), bf16),
            pltpu.VMEM((chunks * 2, NZ, ROWS, wide), bf16),
            pltpu.VMEM((chunks, NZ - 1, 2, ROWS, wide), bf16),
            pltpu.SemaphoreType.DMA((3,)),
            pltpu.SemaphoreType.DMA((copies,)),
            pltpu.SemaphoreType.DMA((copies,)),
        ],
        compiler_params=pltpu.CompilerParams(
            collective_id=0, has_side_effects=True, vmem_limit_bytes=60 * 1024 * 1024
        ),
    )(tokens, wmat, gate_proj[0], up_proj[0], down_proj[0])


def solution(mesh):
    in_specs = (
        P("expert", "hidden"),
        P("expert", None),
        P("expert", None),
        P("expert", "hidden", None),
        P("expert", "hidden", None),
        P("expert", None, "hidden"),
    )
    out_specs = P("expert", "hidden")
    whole_blocks = mesh.shape["expert"] == NZ * NY * NX and mesh.shape["hidden"] == 2
    return jax.shard_map(
        dense if whole_blocks else routed,
        mesh=mesh, in_specs=in_specs, out_specs=out_specs, check_vma=False,
    )
```

```python
import functools

import jax
import jax.numpy as jnp
from jax import lax
from jax.experimental import pallas as pl
from jax.experimental.pallas import tpu as pltpu
from jax.sharding import PartitionSpec as P

MESH = pl.DeviceIdType.MESH
NZ, NY, NX = 4, 2, 2
ROWS = 16
TILE = 256
THIRD = 256


def routed(tokens, expert_ids, gate_weights, gate_proj, up_proj, down_proj):
    local_count = gate_proj.shape[0]
    experts_all = local_count * lax.axis_size("expert")
    tok_rows = tokens.shape[0]
    top_count = expert_ids.shape[1]
    capacity = 2 * tok_rows * top_count // experts_all
    flat_ids = expert_ids.reshape(-1)
    onehot = (flat_ids[:, None] == jnp.arange(experts_all, dtype=jnp.int32)[None, :]).astype(
        jnp.int32
    )
    slot_index = jnp.sum((jnp.cumsum(onehot, axis=0) - onehot) * onehot, axis=1)
    position = flat_ids * capacity + slot_index
    token_of = jnp.arange(tok_rows * top_count, dtype=jnp.int32) // top_count
    full_rows = lax.all_gather(tokens, "hidden", axis=1, tiled=True)
    packed = jnp.zeros((experts_all * capacity, full_rows.shape[1]), full_rows.dtype)
    packed = packed.at[position].set(full_rows[token_of])
    arrived = lax.all_to_all(
        packed.reshape(experts_all, capacity, full_rows.shape[1]),
        "expert",
        split_axis=0,
        concat_axis=1,
        tiled=True,
    )
    gate_sum = jnp.einsum("lrd,lfd->lfr", arrived, gate_proj, preferred_element_type=jnp.float32)
    up_sum = jnp.einsum("lrd,lfd->lfr", arrived, up_proj, preferred_element_type=jnp.float32)
    activation = (jax.nn.silu(gate_sum) * up_sum).astype(jnp.bfloat16)
    expert_out = jnp.einsum(
        "lfr,lfd->lrd",
        lax.all_gather(activation, "hidden", axis=1, tiled=True),
        down_proj,
        preferred_element_type=jnp.float32,
    ).astype(jnp.bfloat16)
    returned = lax.all_to_all(expert_out, "expert", split_axis=1, concat_axis=0, tiled=True)
    gathered = returned.reshape(experts_all * capacity, returned.shape[2])[position]
    gathered = gathered.reshape(tok_rows, top_count, returned.shape[2]).astype(jnp.float32)
    mixed = jnp.sum(gathered * gate_weights[:, :, None], axis=1)
    return mixed.astype(jnp.bfloat16)


def dense_kernel(
    tok_ref, wmat_ref, gate_hbm, up_hbm, down_hbm, out_ref,
    x_buf, xa_buf, w_buf, w_col, gate, up, down, act,
    part, parta, red1, red2, red3, reda1, reda2, reda3,
    local_sem, send_sem, recv_sem,
):
    chunks = tok_ref.shape[0] // ROWS
    wide = x_buf.shape[-1]
    half = tok_ref.shape[1]
    rows = NZ * NY * NX * ROWS
    hid = gate.shape[0]
    f32, bf16 = jnp.float32, jnp.bfloat16
    me = lax.axis_index("expert")
    core = lax.axis_index("hidden")
    z, y, x = me // (NY * NX), (me // NX) % NY, me % NX

    def at(zz, yy, xx):
        return ((zz * NY + yy) * NX + xx, core)

    x_peer, y_peer, sibling = at(z, y, 1 - x), at(z, 1 - y, x), (me, 1 - core)
    z_of = [lax.rem(z + d, NZ) for d in range(NZ)]
    z_peers = [at(z_of[d], y, x) for d in range(NZ)]

    loads = [
        pltpu.make_async_copy(src, dst, local_sem.at[i])
        for i, (src, dst) in enumerate(((gate_hbm, gate), (up_hbm, up), (down_hbm, down)))
    ]
    for load in loads:
        load.start()

    barrier = pltpu.get_barrier_semaphore()
    peers = [x_peer, y_peer, sibling] + z_peers[1:]
    for peer in peers:
        pl.semaphore_signal(barrier, inc=1, device_id=peer, device_id_type=MESH)
    for c in range(chunks):
        for p in range(2):
            x_buf[(c * 2 + core) * 2 + p, z, y, x] = tok_ref[
                c * ROWS : (c + 1) * ROWS, p * wide : (p + 1) * wide
            ]
        xa_buf[c * 2 + core, z, y, x] = tok_ref[c * ROWS : (c + 1) * ROWS, 2 * wide :]
    blank = jnp.zeros((wmat_ref.shape[0], 128 - wmat_ref.shape[1]), f32)
    w_buf[z, y, x] = jnp.concatenate([wmat_ref[...], blank], axis=1)
    pl.semaphore_wait(barrier, len(peers))

    sent = []

    def send(src, dst, peer):
        k = len(sent)
        copy = pltpu.make_async_remote_copy(
            src_ref=src, dst_ref=dst, send_sem=send_sem.at[k], recv_sem=recv_sem.at[k],
            device_id=peer, device_id_type=MESH,
        )
        copy.start()
        sent.append(copy)
        return copy

    def arrive(copies):
        for copy in copies:
            copy.wait_recv()

    def move(ref, peer):
        return send(ref, ref, peer)

    def spread_z(c):
        own = x_buf.at[pl.ds((c * 2 + core) * 2, 2), z, y, x]
        return [move(own, z_peers[d]) for d in range(1, NZ)] + [
            move(xa_buf.at[c * 2 + core, z, y, x], x_peer)
        ]

    def spread_1(c):
        i = (c * 2 + core) * 2
        return [
            move(x_buf.at[i, :, y, x], x_peer),
            move(x_buf.at[i + 1, :, y, x], y_peer),
            move(xa_buf.at[c * 2 + core, z, y], y_peer),
        ]

    def spread_2(c):
        i = (c * 2 + core) * 2
        third = xa_buf.at[c * 2 + core, z]
        return [
            move(x_buf.at[i, :, y], y_peer),
            move(x_buf.at[i + 1, :, :, x], x_peer),
        ] + [move(third, z_peers[d]) for d in range(1, NZ)]

    def spread_core(c):
        return [
            move(x_buf.at[pl.ds((c * 2 + core) * 2, 2)], sibling),
            move(xa_buf.at[c * 2 + core], sibling),
        ]

    def gate_up(c):
        def step(n, carry):
            cols = pl.ds(pl.multiple_of(n * TILE, TILE), TILE)
            sums = []
            for weight in (gate, up):
                total = None
                for k in range(6):
                    hh, p = k // 3, k % 3
                    if p < 2:
                        piece = x_buf[c * 4 + hh * 2 + p].reshape(rows, wide)
                    else:
                        piece = xa_buf[c * 2 + hh].reshape(rows, THIRD)
                    low = hh * half + p * wide
                    term = lax.dot_general(
                        piece,
                        weight[cols, low : low + piece.shape[1]],
                        (((1,), (1,)), ((), ())),
                        preferred_element_type=f32,
                    )
                    total = term if total is None else total + term
                sums.append(total)
            g, u = sums
            act[c * 2 + core, :, cols] = ((g / (1.0 + jnp.exp(-g))) * u).astype(bf16)
            return carry

        lax.fori_loop(0, hid // TILE, step, 0)
        return [move(act.at[c * 2 + core], sibling)]

    def down_tile(c, start, size):
        total = None
        for k in range(2):
            term = jnp.dot(
                act[c * 2 + k], down[k * hid : (k + 1) * hid, pl.ds(start, size)],
                preferred_element_type=f32,
            )
            total = term if total is None else total + term
        scale = w_col[c]
        total = total * jnp.concatenate([scale] * (size // 128), axis=1)
        return total.astype(bf16).reshape(NZ, NY, NX, ROWS, size)

    def down_part(c, p):
        def step(n, carry):
            into = pl.ds(pl.multiple_of(n * TILE, TILE), TILE)
            start = pl.multiple_of(p * wide + n * TILE, 128)
            part[c * 2 + p, :, :, :, :, into] = down_tile(c, start, TILE)
            return carry

        lax.fori_loop(0, wide // TILE, step, 0)
        rest = wide % TILE
        if rest:
            part[c * 2 + p, :, :, :, :, wide - rest :] = down_tile(c, (p + 1) * wide - rest, rest)

    def down_all(c):
        down_part(c, 0)
        first = send(part.at[c * 2, :, 1 - y], red1.at[c * 2], y_peer)
        down_part(c, 1)
        second = send(part.at[c * 2 + 1, :, :, 1 - x], red1.at[c * 2 + 1], x_peer)
        parta[c] = down_tile(c, 2 * wide, THIRD)
        return [first, second] + [
            send(parta.at[c, z_of[d]], reda1.at[c, d - 1], z_peers[d]) for d in range(1, NZ)
        ]

    def reduce_1(c, copies):
        copies[0].wait_recv()
        for zz in range(NZ):
            red1[c * 2, zz] = (
                red1[c * 2, zz].astype(f32) + part[c * 2, zz, y].astype(f32)
            ).astype(bf16)
        first = send(red1.at[c * 2, :, 1 - x], red2.at[c * 2], x_peer)
        copies[1].wait_recv()
        for zz in range(NZ):
            for yy in range(NY):
                red1[c * 2 + 1, zz, yy] = (
                    red1[c * 2 + 1, zz, yy].astype(f32) + part[c * 2 + 1, zz, yy, x].astype(f32)
                ).astype(bf16)
        second = send(red1.at[c * 2 + 1, :, 1 - y], red2.at[c * 2 + 1], y_peer)
        arrive(copies[2:])
        total = parta[c, z].astype(f32)
        for d in range(NZ - 1):
            total = total + reda1[c, d].astype(f32)
        parta[c, z] = total.astype(bf16)
        return [first, second, send(parta.at[c, z, 1 - y], reda2.at[c], y_peer)]

    def reduce_2(c, copies):
        for p, (copy, mine) in enumerate(zip(copies, (x, y))):
            copy.wait_recv()
            for zz in range(NZ):
                red2[c * 2 + p, zz] = (
                    red2[c * 2 + p, zz].astype(f32) + red1[c * 2 + p, zz, mine].astype(f32)
                ).astype(bf16)
        out = [
            send(red2.at[pl.ds(c * 2, 2), z_of[d]], red3.at[c, d - 1], z_peers[d])
            for d in range(1, NZ)
        ]
        copies[2].wait_recv()
        reda2[c] = (reda2[c].astype(f32) + parta[c, z, y].astype(f32)).astype(bf16)
        return out + [send(reda2.at[c, 1 - x], reda3.at[c], x_peer)]

    def finish(c, copies):
        arrive(copies)
        for p in range(2):
            total = red2[c * 2 + p, z].astype(f32)
            for d in range(NZ - 1):
                total = total + red3[c, d, p].astype(f32)
            out_ref[c * ROWS : (c + 1) * ROWS, p * wide : (p + 1) * wide] = total.astype(bf16)
        total = reda2[c, x].astype(f32) + reda3[c].astype(f32)
        out_ref[c * ROWS : (c + 1) * ROWS, 2 * wide :] = total.astype(bf16)

    def columns_of_weights():
        lane = lax.broadcasted_iota(jnp.int32, w_buf.shape[3:], 0)
        picked = [
            jnp.sum(jnp.where(lane == me, w_buf[zz, yy, xx], 0.0), axis=0, keepdims=True)
            for zz in range(NZ) for yy in range(NY) for xx in range(NX)
        ]
        square = jnp.concatenate(picked + [jnp.zeros((128 - len(picked), 128), f32)], axis=0)
        turned = square.T
        for c in range(chunks):
            for b in range(len(picked)):
                w_col[c, b * ROWS : (b + 1) * ROWS, :] = jnp.broadcast_to(
                    turned[c * ROWS : (c + 1) * ROWS, b : b + 1], (ROWS, 128)
                )

    za = [None] * chunks
    s1, s2, sc = [None] * chunks, [None] * chunks, [None] * chunks
    aa, r1, r2, r3 = [None] * chunks, [None] * chunks, [None] * chunks, [None] * chunks

    za[0] = spread_z(0)
    wz = [move(w_buf.at[z, y, x], z_peers[d]) for d in range(1, NZ)]
    za[1] = spread_z(1)
    arrive(za[0])
    s1[0] = spread_1(0)
    arrive(wz)
    wx = [move(w_buf.at[:, y, x], x_peer)]
    za[2] = spread_z(2)
    arrive(s1[0])
    s2[0] = spread_2(0)
    arrive(wx)
    wy = [move(w_buf.at[:, y], y_peer)]
    arrive(za[1])
    s1[1] = spread_1(1)
    za[3] = spread_z(3)
    arrive(s1[1])
    s2[1] = spread_2(1)
    arrive(wy)
    columns_of_weights()
    arrive(s2[0])
    sc[0] = spread_core(0)
    arrive(za[2])
    s1[2] = spread_1(2)
    loads[0].wait()
    loads[1].wait()
    loads[2].wait()
    arrive(sc[0])
    aa[0] = gate_up(0)
    arrive(s1[2])
    s2[2] = spread_2(2)
    arrive(s2[1])
    sc[1] = spread_core(1)
    arrive(za[3])
    s1[3] = spread_1(3)
    arrive(sc[1])
    aa[1] = gate_up(1)
    arrive(s1[3])
    s2[3] = spread_2(3)
    arrive(aa[0])
    r1[0] = down_all(0)
    arrive(s2[2])
    sc[2] = spread_core(2)
    arrive(aa[1])
    r1[1] = down_all(1)
    arrive(sc[2])
    aa[2] = gate_up(2)
    r2[0] = reduce_1(0, r1[0])
    arrive(s2[3])
    sc[3] = spread_core(3)
    arrive(aa[2])
    r1[2] = down_all(2)
    arrive(sc[3])
    aa[3] = gate_up(3)
    r2[1] = reduce_1(1, r1[1])
    r3[0] = reduce_2(0, r2[0])
    arrive(aa[3])
    r1[3] = down_all(3)
    r2[2] = reduce_1(2, r1[2])
    r3[1] = reduce_2(1, r2[1])
    finish(0, r3[0])
    r2[3] = reduce_1(3, r1[3])
    r3[2] = reduce_2(2, r2[2])
    finish(1, r3[1])
    r3[3] = reduce_2(3, r2[3])
    finish(2, r3[2])
    finish(3, r3[3])
    for copy in sent:
        copy.wait_send()


def dense(tokens, expert_ids, gate_weights, gate_proj, up_proj, down_proj):
    tok_rows, half = tokens.shape
    experts_all = lax.axis_size("expert")
    hid, width = gate_proj.shape[1:]
    chunks = tok_rows // ROWS
    wide = (half - THIRD) // 2
    rows = experts_all * ROWS
    chosen = expert_ids[None, :, :] == jnp.arange(experts_all, dtype=jnp.int32)[:, None, None]
    wmat = jnp.sum(jnp.where(chosen, gate_weights[None], 0.0), axis=2)
    bf16, f32 = jnp.bfloat16, jnp.float32
    vmem = pl.BlockSpec(memory_space=pltpu.VMEM)
    hbm = pl.BlockSpec(memory_space=pl.ANY)
    copies = chunks * 27 + 5
    return pl.pallas_call(
        dense_kernel,
        out_shape=jax.ShapeDtypeStruct((tok_rows, half), bf16),
        in_specs=[vmem, vmem, hbm, hbm, hbm],
        out_specs=vmem,
        scratch_shapes=[
            pltpu.VMEM((chunks * 4, NZ, NY, NX, ROWS, wide), bf16),
            pltpu.VMEM((chunks * 2, NZ, NY, NX, ROWS, THIRD), bf16),
            pltpu.VMEM((NZ, NY, NX, experts_all, 128), f32),
            pltpu.VMEM((chunks, rows, 128), f32),
            pltpu.VMEM((hid, width), bf16),
            pltpu.VMEM((hid, width), bf16),
            pltpu.VMEM((2 * hid, half), bf16),
            pltpu.VMEM((chunks * 2, rows, hid), bf16),
            pltpu.VMEM((chunks * 2, NZ, NY, NX, ROWS, wide), bf16),
            pltpu.VMEM((chunks, NZ, NY, NX, ROWS, THIRD), bf16),
            pltpu.VMEM((chunks * 2, NZ, 2, ROWS, wide), bf16),
            pltpu.VMEM((chunks * 2, NZ, ROWS, wide), bf16),
            pltpu.VMEM((chunks, NZ - 1, 2, ROWS, wide), bf16),
            pltpu.VMEM((chunks, NZ - 1, NY, NX, ROWS, THIRD), bf16),
            pltpu.VMEM((chunks, NX, ROWS, THIRD), bf16),
            pltpu.VMEM((chunks, ROWS, THIRD), bf16),
            pltpu.SemaphoreType.DMA((3,)),
            pltpu.SemaphoreType.DMA((copies,)),
            pltpu.SemaphoreType.DMA((copies,)),
        ],
        compiler_params=pltpu.CompilerParams(
            collective_id=0, has_side_effects=True, vmem_limit_bytes=60 * 1024 * 1024
        ),
    )(tokens, wmat, gate_proj[0], up_proj[0], down_proj[0])


def solution(mesh):
    in_specs = (
        P("expert", "hidden"),
        P("expert", None),
        P("expert", None),
        P("expert", "hidden", None),
        P("expert", "hidden", None),
        P("expert", None, "hidden"),
    )
    out_specs = P("expert", "hidden")
    whole_blocks = mesh.shape["expert"] == NZ * NY * NX and mesh.shape["hidden"] == 2
    return jax.shard_map(
        dense if whole_blocks else routed,
        mesh=mesh, in_specs=in_specs, out_specs=out_specs, check_vma=False,
    )
```

```python
import functools

import jax
import jax.numpy as jnp
from jax import lax
from jax.experimental import pallas as pl
from jax.experimental.pallas import tpu as pltpu
from jax.sharding import PartitionSpec as P

MESH = pl.DeviceIdType.MESH
NZ, NY, NX = 4, 2, 2
ROWS = 16
TILE = 256
THIRD = 256


def routed(tokens, expert_ids, gate_weights, gate_proj, up_proj, down_proj):
    local_count = gate_proj.shape[0]
    experts_all = local_count * lax.axis_size("expert")
    tok_rows = tokens.shape[0]
    top_count = expert_ids.shape[1]
    capacity = 2 * tok_rows * top_count // experts_all
    flat_ids = expert_ids.reshape(-1)
    onehot = (flat_ids[:, None] == jnp.arange(experts_all, dtype=jnp.int32)[None, :]).astype(
        jnp.int32
    )
    slot_index = jnp.sum((jnp.cumsum(onehot, axis=0) - onehot) * onehot, axis=1)
    position = flat_ids * capacity + slot_index
    token_of = jnp.arange(tok_rows * top_count, dtype=jnp.int32) // top_count
    full_rows = lax.all_gather(tokens, "hidden", axis=1, tiled=True)
    packed = jnp.zeros((experts_all * capacity, full_rows.shape[1]), full_rows.dtype)
    packed = packed.at[position].set(full_rows[token_of])
    arrived = lax.all_to_all(
        packed.reshape(experts_all, capacity, full_rows.shape[1]),
        "expert",
        split_axis=0,
        concat_axis=1,
        tiled=True,
    )
    gate_sum = jnp.einsum("lrd,lfd->lfr", arrived, gate_proj, preferred_element_type=jnp.float32)
    up_sum = jnp.einsum("lrd,lfd->lfr", arrived, up_proj, preferred_element_type=jnp.float32)
    activation = (jax.nn.silu(gate_sum) * up_sum).astype(jnp.bfloat16)
    expert_out = jnp.einsum(
        "lfr,lfd->lrd",
        lax.all_gather(activation, "hidden", axis=1, tiled=True),
        down_proj,
        preferred_element_type=jnp.float32,
    ).astype(jnp.bfloat16)
    returned = lax.all_to_all(expert_out, "expert", split_axis=1, concat_axis=0, tiled=True)
    gathered = returned.reshape(experts_all * capacity, returned.shape[2])[position]
    gathered = gathered.reshape(tok_rows, top_count, returned.shape[2]).astype(jnp.float32)
    mixed = jnp.sum(gathered * gate_weights[:, :, None], axis=1)
    return mixed.astype(jnp.bfloat16)


def dense_kernel(
    tok_ref, wmat_ref, gate_hbm, up_hbm, down_hbm, out_ref,
    x_buf, xa_buf, w_buf, w_col, gate, up, down, act,
    part, parta, red1, red2, red3, reda1, reda2, reda3,
    local_sem, send_sem, recv_sem,
):
    chunks = tok_ref.shape[0] // ROWS
    wide = x_buf.shape[-1]
    half = tok_ref.shape[1]
    rows = NZ * NY * NX * ROWS
    hid = gate.shape[0]
    f32, bf16 = jnp.float32, jnp.bfloat16
    me = lax.axis_index("expert")
    core = lax.axis_index("hidden")
    z, y, x = me // (NY * NX), (me // NX) % NY, me % NX

    def at(zz, yy, xx):
        return ((zz * NY + yy) * NX + xx, core)

    x_peer, y_peer, sibling = at(z, y, 1 - x), at(z, 1 - y, x), (me, 1 - core)
    z_of = [lax.rem(z + d, NZ) for d in range(NZ)]
    z_peers = [at(z_of[d], y, x) for d in range(NZ)]

    loads = [
        pltpu.make_async_copy(src, dst, local_sem.at[i])
        for i, (src, dst) in enumerate(((gate_hbm, gate), (up_hbm, up), (down_hbm, down)))
    ]
    for load in loads:
        load.start()

    barrier = pltpu.get_barrier_semaphore()
    peers = [x_peer, y_peer, sibling] + z_peers[1:]
    for peer in peers:
        pl.semaphore_signal(barrier, inc=1, device_id=peer, device_id_type=MESH)
    for c in range(chunks):
        for p in range(2):
            x_buf[(c * 2 + core) * 2 + p, z, y, x] = tok_ref[
                c * ROWS : (c + 1) * ROWS, p * wide : (p + 1) * wide
            ]
        xa_buf[c * 2 + core, z, y, x] = tok_ref[c * ROWS : (c + 1) * ROWS, 2 * wide :]
    blank = jnp.zeros((wmat_ref.shape[0], 128 - wmat_ref.shape[1]), f32)
    w_buf[z, y, x] = jnp.concatenate([wmat_ref[...], blank], axis=1)
    pl.semaphore_wait(barrier, len(peers))

    sent = []

    def send(src, dst, peer):
        k = len(sent)
        copy = pltpu.make_async_remote_copy(
            src_ref=src, dst_ref=dst, send_sem=send_sem.at[k], recv_sem=recv_sem.at[k],
            device_id=peer, device_id_type=MESH,
        )
        copy.start()
        sent.append(copy)
        return copy

    def arrive(copies):
        for copy in copies:
            copy.wait_recv()

    def move(ref, peer):
        return send(ref, ref, peer)

    def spread_z(c):
        own = x_buf.at[pl.ds((c * 2 + core) * 2, 2), z, y, x]
        return [move(own, z_peers[d]) for d in range(1, NZ)] + [
            move(xa_buf.at[c * 2 + core, z, y, x], x_peer)
        ]

    def spread_1(c):
        i = (c * 2 + core) * 2
        return [
            move(x_buf.at[i, :, y, x], x_peer),
            move(x_buf.at[i + 1, :, y, x], y_peer),
            move(xa_buf.at[c * 2 + core, z, y], y_peer),
        ]

    def spread_2(c):
        i = (c * 2 + core) * 2
        third = xa_buf.at[c * 2 + core, z]
        return [
            move(x_buf.at[i, :, y], y_peer),
            move(x_buf.at[i + 1, :, :, x], x_peer),
        ] + [move(third, z_peers[d]) for d in range(1, NZ)]

    def spread_core(c):
        return [
            move(x_buf.at[pl.ds((c * 2 + core) * 2, 2)], sibling),
            move(xa_buf.at[c * 2 + core], sibling),
        ]

    def gate_up(c):
        sums = []
        for weight in (gate, up):
            total = None
            for k in range(6):
                hh, p = k // 3, k % 3
                if p < 2:
                    piece = x_buf[c * 4 + hh * 2 + p].reshape(rows, wide)
                else:
                    piece = xa_buf[c * 2 + hh].reshape(rows, THIRD)
                low = hh * half + p * wide
                term = lax.dot_general(
                    weight[:, low : low + piece.shape[1]],
                    piece,
                    (((1,), (1,)), ((), ())),
                    preferred_element_type=f32,
                )
                total = term if total is None else total + term
            sums.append(total)
        g, u = sums
        act[c * 2 + core] = ((g / (1.0 + jnp.exp(-g))) * u).T.astype(bf16)
        return [move(act.at[c * 2 + core], sibling)]

    def down_tile(c, start, size):
        total = None
        for k in range(2):
            term = jnp.dot(
                act[c * 2 + k], down[k * hid : (k + 1) * hid, pl.ds(start, size)],
                preferred_element_type=f32,
            )
            total = term if total is None else total + term
        scale = w_col[c]
        total = total * jnp.concatenate([scale] * (size // 128), axis=1)
        return total.astype(bf16).reshape(NZ, NY, NX, ROWS, size)

    def down_part(c, p):
        def step(n, carry):
            into = pl.ds(pl.multiple_of(n * TILE, TILE), TILE)
            start = pl.multiple_of(p * wide + n * TILE, 128)
            part[c * 2 + p, :, :, :, :, into] = down_tile(c, start, TILE)
            return carry

        lax.fori_loop(0, wide // TILE, step, 0)
        rest = wide % TILE
        if rest:
            part[c * 2 + p, :, :, :, :, wide - rest :] = down_tile(c, (p + 1) * wide - rest, rest)

    def down_all(c):
        down_part(c, 0)
        first = send(part.at[c * 2, :, 1 - y], red1.at[c * 2], y_peer)
        down_part(c, 1)
        second = send(part.at[c * 2 + 1, :, :, 1 - x], red1.at[c * 2 + 1], x_peer)
        parta[c] = down_tile(c, 2 * wide, THIRD)
        return [first, second] + [
            send(parta.at[c, z_of[d]], reda1.at[c, d - 1], z_peers[d]) for d in range(1, NZ)
        ]

    def reduce_1(c, copies):
        copies[0].wait_recv()
        for zz in range(NZ):
            red1[c * 2, zz] = (
                red1[c * 2, zz].astype(f32) + part[c * 2, zz, y].astype(f32)
            ).astype(bf16)
        first = send(red1.at[c * 2, :, 1 - x], red2.at[c * 2], x_peer)
        copies[1].wait_recv()
        for zz in range(NZ):
            for yy in range(NY):
                red1[c * 2 + 1, zz, yy] = (
                    red1[c * 2 + 1, zz, yy].astype(f32) + part[c * 2 + 1, zz, yy, x].astype(f32)
                ).astype(bf16)
        second = send(red1.at[c * 2 + 1, :, 1 - y], red2.at[c * 2 + 1], y_peer)
        arrive(copies[2:])
        total = parta[c, z].astype(f32)
        for d in range(NZ - 1):
            total = total + reda1[c, d].astype(f32)
        parta[c, z] = total.astype(bf16)
        return [first, second, send(parta.at[c, z, 1 - y], reda2.at[c], y_peer)]

    def reduce_2(c, copies):
        for p, (copy, mine) in enumerate(zip(copies, (x, y))):
            copy.wait_recv()
            for zz in range(NZ):
                red2[c * 2 + p, zz] = (
                    red2[c * 2 + p, zz].astype(f32) + red1[c * 2 + p, zz, mine].astype(f32)
                ).astype(bf16)
        out = [
            send(red2.at[pl.ds(c * 2, 2), z_of[d]], red3.at[c, d - 1], z_peers[d])
            for d in range(1, NZ)
        ]
        copies[2].wait_recv()
        reda2[c] = (reda2[c].astype(f32) + parta[c, z, y].astype(f32)).astype(bf16)
        return out + [send(reda2.at[c, 1 - x], reda3.at[c], x_peer)]

    def finish(c, copies):
        arrive(copies)
        for p in range(2):
            total = red2[c * 2 + p, z].astype(f32)
            for d in range(NZ - 1):
                total = total + red3[c, d, p].astype(f32)
            out_ref[c * ROWS : (c + 1) * ROWS, p * wide : (p + 1) * wide] = total.astype(bf16)
        total = reda2[c, x].astype(f32) + reda3[c].astype(f32)
        out_ref[c * ROWS : (c + 1) * ROWS, 2 * wide :] = total.astype(bf16)

    def columns_of_weights():
        lane = lax.broadcasted_iota(jnp.int32, w_buf.shape[3:], 0)
        picked = [
            jnp.sum(jnp.where(lane == me, w_buf[zz, yy, xx], 0.0), axis=0, keepdims=True)
            for zz in range(NZ) for yy in range(NY) for xx in range(NX)
        ]
        square = jnp.concatenate(picked + [jnp.zeros((128 - len(picked), 128), f32)], axis=0)
        turned = square.T
        for c in range(chunks):
            for b in range(len(picked)):
                w_col[c, b * ROWS : (b + 1) * ROWS, :] = jnp.broadcast_to(
                    turned[c * ROWS : (c + 1) * ROWS, b : b + 1], (ROWS, 128)
                )

    za = [None] * chunks
    s1, s2, sc = [None] * chunks, [None] * chunks, [None] * chunks
    aa, r1, r2, r3 = [None] * chunks, [None] * chunks, [None] * chunks, [None] * chunks

    za[0] = spread_z(0)
    wz = [move(w_buf.at[z, y, x], z_peers[d]) for d in range(1, NZ)]
    za[1] = spread_z(1)
    arrive(za[0])
    s1[0] = spread_1(0)
    arrive(wz)
    wx = [move(w_buf.at[:, y, x], x_peer)]
    za[2] = spread_z(2)
    arrive(s1[0])
    s2[0] = spread_2(0)
    arrive(wx)
    wy = [move(w_buf.at[:, y], y_peer)]
    arrive(za[1])
    s1[1] = spread_1(1)
    za[3] = spread_z(3)
    arrive(s1[1])
    s2[1] = spread_2(1)
    arrive(wy)
    columns_of_weights()
    arrive(s2[0])
    sc[0] = spread_core(0)
    arrive(za[2])
    s1[2] = spread_1(2)
    loads[0].wait()
    loads[1].wait()
    loads[2].wait()
    arrive(sc[0])
    aa[0] = gate_up(0)
    arrive(s1[2])
    s2[2] = spread_2(2)
    arrive(s2[1])
    sc[1] = spread_core(1)
    arrive(za[3])
    s1[3] = spread_1(3)
    arrive(sc[1])
    aa[1] = gate_up(1)
    arrive(s1[3])
    s2[3] = spread_2(3)
    arrive(aa[0])
    r1[0] = down_all(0)
    arrive(s2[2])
    sc[2] = spread_core(2)
    arrive(aa[1])
    r1[1] = down_all(1)
    arrive(sc[2])
    aa[2] = gate_up(2)
    r2[0] = reduce_1(0, r1[0])
    arrive(s2[3])
    sc[3] = spread_core(3)
    arrive(aa[2])
    r1[2] = down_all(2)
    arrive(sc[3])
    aa[3] = gate_up(3)
    r2[1] = reduce_1(1, r1[1])
    r3[0] = reduce_2(0, r2[0])
    arrive(aa[3])
    r1[3] = down_all(3)
    r2[2] = reduce_1(2, r1[2])
    r3[1] = reduce_2(1, r2[1])
    finish(0, r3[0])
    r2[3] = reduce_1(3, r1[3])
    r3[2] = reduce_2(2, r2[2])
    finish(1, r3[1])
    r3[3] = reduce_2(3, r2[3])
    finish(2, r3[2])
    finish(3, r3[3])
    for copy in sent:
        copy.wait_send()


def dense(tokens, expert_ids, gate_weights, gate_proj, up_proj, down_proj):
    tok_rows, half = tokens.shape
    experts_all = lax.axis_size("expert")
    hid, width = gate_proj.shape[1:]
    chunks = tok_rows // ROWS
    wide = (half - THIRD) // 2
    rows = experts_all * ROWS
    chosen = expert_ids[None, :, :] == jnp.arange(experts_all, dtype=jnp.int32)[:, None, None]
    wmat = jnp.sum(jnp.where(chosen, gate_weights[None], 0.0), axis=2)
    bf16, f32 = jnp.bfloat16, jnp.float32
    vmem = pl.BlockSpec(memory_space=pltpu.VMEM)
    hbm = pl.BlockSpec(memory_space=pl.ANY)
    copies = chunks * 27 + 5
    return pl.pallas_call(
        dense_kernel,
        out_shape=jax.ShapeDtypeStruct((tok_rows, half), bf16),
        in_specs=[vmem, vmem, hbm, hbm, hbm],
        out_specs=vmem,
        scratch_shapes=[
            pltpu.VMEM((chunks * 4, NZ, NY, NX, ROWS, wide), bf16),
            pltpu.VMEM((chunks * 2, NZ, NY, NX, ROWS, THIRD), bf16),
            pltpu.VMEM((NZ, NY, NX, experts_all, 128), f32),
            pltpu.VMEM((chunks, rows, 128), f32),
            pltpu.VMEM((hid, width), bf16),
            pltpu.VMEM((hid, width), bf16),
            pltpu.VMEM((2 * hid, half), bf16),
            pltpu.VMEM((chunks * 2, rows, hid), bf16),
            pltpu.VMEM((chunks * 2, NZ, NY, NX, ROWS, wide), bf16),
            pltpu.VMEM((chunks, NZ, NY, NX, ROWS, THIRD), bf16),
            pltpu.VMEM((chunks * 2, NZ, 2, ROWS, wide), bf16),
            pltpu.VMEM((chunks * 2, NZ, ROWS, wide), bf16),
            pltpu.VMEM((chunks, NZ - 1, 2, ROWS, wide), bf16),
            pltpu.VMEM((chunks, NZ - 1, NY, NX, ROWS, THIRD), bf16),
            pltpu.VMEM((chunks, NX, ROWS, THIRD), bf16),
            pltpu.VMEM((chunks, ROWS, THIRD), bf16),
            pltpu.SemaphoreType.DMA((3,)),
            pltpu.SemaphoreType.DMA((copies,)),
            pltpu.SemaphoreType.DMA((copies,)),
        ],
        compiler_params=pltpu.CompilerParams(
            collective_id=0, has_side_effects=True, vmem_limit_bytes=60 * 1024 * 1024
        ),
    )(tokens, wmat, gate_proj[0], up_proj[0], down_proj[0])


def solution(mesh):
    in_specs = (
        P("expert", "hidden"),
        P("expert", None),
        P("expert", None),
        P("expert", "hidden", None),
        P("expert", "hidden", None),
        P("expert", None, "hidden"),
    )
    out_specs = P("expert", "hidden")
    whole_blocks = mesh.shape["expert"] == NZ * NY * NX and mesh.shape["hidden"] == 2
    return jax.shard_map(
        dense if whole_blocks else routed,
        mesh=mesh, in_specs=in_specs, out_specs=out_specs, check_vma=False,
    )
```

```python
import functools

import jax
import jax.numpy as jnp
from jax import lax
from jax.experimental import pallas as pl
from jax.experimental.pallas import tpu as pltpu
from jax.sharding import PartitionSpec as P

MESH = pl.DeviceIdType.MESH
NZ, NY, NX = 4, 2, 2
ROWS = 16
TILE = 256
THIRD = 256


def routed(tokens, expert_ids, gate_weights, gate_proj, up_proj, down_proj):
    local_count = gate_proj.shape[0]
    experts_all = local_count * lax.axis_size("expert")
    tok_rows = tokens.shape[0]
    top_count = expert_ids.shape[1]
    capacity = 2 * tok_rows * top_count // experts_all
    flat_ids = expert_ids.reshape(-1)
    onehot = (flat_ids[:, None] == jnp.arange(experts_all, dtype=jnp.int32)[None, :]).astype(
        jnp.int32
    )
    slot_index = jnp.sum((jnp.cumsum(onehot, axis=0) - onehot) * onehot, axis=1)
    position = flat_ids * capacity + slot_index
    token_of = jnp.arange(tok_rows * top_count, dtype=jnp.int32) // top_count
    full_rows = lax.all_gather(tokens, "hidden", axis=1, tiled=True)
    packed = jnp.zeros((experts_all * capacity, full_rows.shape[1]), full_rows.dtype)
    packed = packed.at[position].set(full_rows[token_of])
    arrived = lax.all_to_all(
        packed.reshape(experts_all, capacity, full_rows.shape[1]),
        "expert",
        split_axis=0,
        concat_axis=1,
        tiled=True,
    )
    gate_sum = jnp.einsum("lrd,lfd->lfr", arrived, gate_proj, preferred_element_type=jnp.float32)
    up_sum = jnp.einsum("lrd,lfd->lfr", arrived, up_proj, preferred_element_type=jnp.float32)
    activation = (jax.nn.silu(gate_sum) * up_sum).astype(jnp.bfloat16)
    expert_out = jnp.einsum(
        "lfr,lfd->lrd",
        lax.all_gather(activation, "hidden", axis=1, tiled=True),
        down_proj,
        preferred_element_type=jnp.float32,
    ).astype(jnp.bfloat16)
    returned = lax.all_to_all(expert_out, "expert", split_axis=1, concat_axis=0, tiled=True)
    gathered = returned.reshape(experts_all * capacity, returned.shape[2])[position]
    gathered = gathered.reshape(tok_rows, top_count, returned.shape[2]).astype(jnp.float32)
    mixed = jnp.sum(gathered * gate_weights[:, :, None], axis=1)
    return mixed.astype(jnp.bfloat16)


def dense_kernel(
    tok_ref, ids_ref, weight_ref, gate_hbm, up_hbm, down_hbm, out_ref,
    x_buf, xa_buf, w_buf, w_col, gate, up, down, act,
    part, parta, red1, red2, red3, reda1, reda2, reda3,
    local_sem, send_sem, recv_sem,
):
    chunks = tok_ref.shape[0] // ROWS
    wide = x_buf.shape[-1]
    half = tok_ref.shape[1]
    rows = NZ * NY * NX * ROWS
    hid = gate.shape[0]
    f32, bf16 = jnp.float32, jnp.bfloat16
    me = lax.axis_index("expert")
    core = lax.axis_index("hidden")
    z, y, x = me // (NY * NX), (me // NX) % NY, me % NX

    def at(zz, yy, xx):
        return ((zz * NY + yy) * NX + xx, core)

    x_peer, y_peer, sibling = at(z, y, 1 - x), at(z, 1 - y, x), (me, 1 - core)
    z_of = [lax.rem(z + d, NZ) for d in range(NZ)]
    z_peers = [at(z_of[d], y, x) for d in range(NZ)]

    loads = [
        pltpu.make_async_copy(src, dst, local_sem.at[i])
        for i, (src, dst) in enumerate(((gate_hbm, gate), (up_hbm, up), (down_hbm, down)))
    ]
    for load in loads:
        load.start()

    barrier = pltpu.get_barrier_semaphore()
    peers = [x_peer, y_peer, sibling] + z_peers[1:]
    for peer in peers:
        pl.semaphore_signal(barrier, inc=1, device_id=peer, device_id_type=MESH)
    for c in range(chunks):
        for p in range(2):
            x_buf[(c * 2 + core) * 2 + p, z, y, x] = tok_ref[
                c * ROWS : (c + 1) * ROWS, p * wide : (p + 1) * wide
            ]
        xa_buf[c * 2 + core, z, y, x] = tok_ref[c * ROWS : (c + 1) * ROWS, 2 * wide :]
    tok_rows = tok_ref.shape[0]
    lane = lax.broadcasted_iota(jnp.int32, (tok_rows, 128), 1)
    table = jnp.zeros((tok_rows, 128), f32)
    for k in range(ids_ref.shape[1]):
        table = table + jnp.where(ids_ref[:, k : k + 1] == lane, weight_ref[:, k : k + 1], 0.0)
    table = jnp.concatenate([table, jnp.zeros((128 - tok_rows, 128), f32)], axis=0)
    w_buf[z, y, x] = table.T[: w_buf.shape[3]]
    pl.semaphore_wait(barrier, len(peers))

    sent = []

    def send(src, dst, peer):
        k = len(sent)
        copy = pltpu.make_async_remote_copy(
            src_ref=src, dst_ref=dst, send_sem=send_sem.at[k], recv_sem=recv_sem.at[k],
            device_id=peer, device_id_type=MESH,
        )
        copy.start()
        sent.append(copy)
        return copy

    def arrive(copies):
        for copy in copies:
            copy.wait_recv()

    def move(ref, peer):
        return send(ref, ref, peer)

    def spread_z(c):
        own = x_buf.at[pl.ds((c * 2 + core) * 2, 2), z, y, x]
        return [move(own, z_peers[d]) for d in range(1, NZ)] + [
            move(xa_buf.at[c * 2 + core, z, y, x], x_peer)
        ]

    def spread_1(c):
        i = (c * 2 + core) * 2
        return [
            move(x_buf.at[i, :, y, x], x_peer),
            move(x_buf.at[i + 1, :, y, x], y_peer),
            move(xa_buf.at[c * 2 + core, z, y], y_peer),
        ]

    def spread_1_first(c, copies):
        i = (c * 2 + core) * 2

        def pair(zz):
            return [
                move(x_buf.at[i, zz, y, x], x_peer),
                move(x_buf.at[i + 1, zz, y, x], y_peer),
            ]

        out = pair(z)
        for d in range(1, NZ):
            copies[d - 1].wait_recv()
            out = out + pair(z_of[NZ - d])
        copies[NZ - 1].wait_recv()
        return out + [move(xa_buf.at[c * 2 + core, z, y], y_peer)]

    def spread_2(c):
        i = (c * 2 + core) * 2
        third = xa_buf.at[c * 2 + core, z]
        return [
            move(x_buf.at[i, :, y], y_peer),
            move(x_buf.at[i + 1, :, :, x], x_peer),
        ] + [move(third, z_peers[d]) for d in range(1, NZ)]

    def spread_core(c):
        return [
            move(x_buf.at[pl.ds((c * 2 + core) * 2, 2)], sibling),
            move(xa_buf.at[c * 2 + core], sibling),
        ]

    def gate_up(c, between):
        sums = []
        for weight in (gate, up):
            if sums:
                between()
            total = None
            for k in range(6):
                hh, p = k // 3, k % 3
                if p < 2:
                    piece = x_buf[c * 4 + hh * 2 + p].reshape(rows, wide)
                else:
                    piece = xa_buf[c * 2 + hh].reshape(rows, THIRD)
                low = hh * half + p * wide
                term = lax.dot_general(
                    weight[:, low : low + piece.shape[1]],
                    piece,
                    (((1,), (1,)), ((), ())),
                    preferred_element_type=f32,
                )
                total = term if total is None else total + term
            sums.append(total)
        g, u = sums
        act[c * 2 + core] = ((g / (1.0 + jnp.exp(-g))) * u).T.astype(bf16)
        return [move(act.at[c * 2 + core], sibling)]

    def down_tile(c, start, size):
        total = None
        for k in range(2):
            term = jnp.dot(
                act[c * 2 + k], down[k * hid : (k + 1) * hid, pl.ds(start, size)],
                preferred_element_type=f32,
            )
            total = term if total is None else total + term
        scale = w_col[c]
        total = total * jnp.concatenate([scale] * (size // 128), axis=1)
        return total.astype(bf16).reshape(NZ, NY, NX, ROWS, size)

    def down_part(c, p):
        def step(n, carry):
            into = pl.ds(pl.multiple_of(n * TILE, TILE), TILE)
            start = pl.multiple_of(p * wide + n * TILE, 128)
            part[c * 2 + p, :, :, :, :, into] = down_tile(c, start, TILE)
            return carry

        lax.fori_loop(0, wide // TILE, step, 0)
        rest = wide % TILE
        if rest:
            part[c * 2 + p, :, :, :, :, wide - rest :] = down_tile(c, (p + 1) * wide - rest, rest)

    def down_all(c):
        down_part(c, 0)
        first = send(part.at[c * 2, :, 1 - y], red1.at[c * 2], y_peer)
        down_part(c, 1)
        second = send(part.at[c * 2 + 1, :, :, 1 - x], red1.at[c * 2 + 1], x_peer)
        parta[c] = down_tile(c, 2 * wide, THIRD)
        return [first, second] + [
            send(parta.at[c, z_of[d]], reda1.at[c, d - 1], z_peers[d]) for d in range(1, NZ)
        ]

    def reduce_1(c, copies):
        copies[0].wait_recv()
        for zz in range(NZ):
            red1[c * 2, zz] = (
                red1[c * 2, zz].astype(f32) + part[c * 2, zz, y].astype(f32)
            ).astype(bf16)
        first = send(red1.at[c * 2, :, 1 - x], red2.at[c * 2], x_peer)
        copies[1].wait_recv()
        for zz in range(NZ):
            for yy in range(NY):
                red1[c * 2 + 1, zz, yy] = (
                    red1[c * 2 + 1, zz, yy].astype(f32) + part[c * 2 + 1, zz, yy, x].astype(f32)
                ).astype(bf16)
        second = send(red1.at[c * 2 + 1, :, 1 - y], red2.at[c * 2 + 1], y_peer)
        arrive(copies[2:])
        total = parta[c, z].astype(f32)
        for d in range(NZ - 1):
            total = total + reda1[c, d].astype(f32)
        parta[c, z] = total.astype(bf16)
        return [first, second, send(parta.at[c, z, 1 - y], reda2.at[c], y_peer)]

    def reduce_2(c, copies):
        out = []
        for p, (copy, mine) in enumerate(zip(copies, (x, y))):
            copy.wait_recv()
            for d in (1, 2, 3, 0):
                zz = z_of[d]
                red2[c * 2 + p, zz] = (
                    red2[c * 2 + p, zz].astype(f32) + red1[c * 2 + p, zz, mine].astype(f32)
                ).astype(bf16)
                if d:
                    out.append(send(red2.at[c * 2 + p, zz], red3.at[c, d - 1, p], z_peers[d]))
        copies[2].wait_recv()
        reda2[c] = (reda2[c].astype(f32) + parta[c, z, y].astype(f32)).astype(bf16)
        return out + [send(reda2.at[c, 1 - x], reda3.at[c], x_peer)]

    def finish(c, copies):
        arrive(copies)
        for p in range(2):
            total = red2[c * 2 + p, z].astype(f32)
            for d in range(NZ - 1):
                total = total + red3[c, d, p].astype(f32)
            out_ref[c * ROWS : (c + 1) * ROWS, p * wide : (p + 1) * wide] = total.astype(bf16)
        total = reda2[c, x].astype(f32) + reda3[c].astype(f32)
        out_ref[c * ROWS : (c + 1) * ROWS, 2 * wide :] = total.astype(bf16)

    def columns_of_weights():
        lane = lax.broadcasted_iota(jnp.int32, w_buf.shape[3:], 0)
        picked = [
            jnp.sum(jnp.where(lane == me, w_buf[zz, yy, xx], 0.0), axis=0, keepdims=True)
            for zz in range(NZ) for yy in range(NY) for xx in range(NX)
        ]
        square = jnp.concatenate(picked + [jnp.zeros((128 - len(picked), 128), f32)], axis=0)
        turned = square.T
        for c in range(chunks):
            for b in range(len(picked)):
                w_col[c, b * ROWS : (b + 1) * ROWS, :] = jnp.broadcast_to(
                    turned[c * ROWS : (c + 1) * ROWS, b : b + 1], (ROWS, 128)
                )

    za = [None] * chunks
    s1, s2, sc = [None] * chunks, [None] * chunks, [None] * chunks
    aa, r1, r2, r3 = [None] * chunks, [None] * chunks, [None] * chunks, [None] * chunks

    za[0] = spread_z(0)
    s1[0] = spread_1_first(0, za[0])
    wz = [move(w_buf.at[z, y, x], z_peers[d]) for d in range(1, NZ)]
    za[1] = spread_z(1)
    arrive(s1[0])
    s2[0] = spread_2(0)
    arrive(wz)
    wx = [move(w_buf.at[:, y, x], x_peer)]
    arrive(za[1])
    s1[1] = spread_1(1)
    za[2] = spread_z(2)
    arrive(wx)
    wy = [move(w_buf.at[:, y], y_peer)]
    arrive(s1[1])
    s2[1] = spread_2(1)
    za[3] = spread_z(3)
    arrive(wy)
    columns_of_weights()
    arrive(s2[0])
    sc[0] = spread_core(0)
    arrive(za[2])
    s1[2] = spread_1(2)
    for load in loads:
        load.wait()
    arrive(sc[0])

    def between_0():
        arrive(s1[2])
        s2[2] = spread_2(2)
        arrive(za[3])
        s1[3] = spread_1(3)

    def between_1():
        arrive(s1[3])
        s2[3] = spread_2(3)

    def between_2():
        arrive(s2[3])
        sc[3] = spread_core(3)
        r2[0] = reduce_1(0, r1[0])

    def between_3():
        r2[1] = reduce_1(1, r1[1])
        r3[0] = reduce_2(0, r2[0])

    aa[0] = gate_up(0, between_0)
    arrive(s2[1])
    sc[1] = spread_core(1)
    arrive(sc[1])
    aa[1] = gate_up(1, between_1)
    arrive(aa[0])
    r1[0] = down_all(0)
    arrive(s2[2])
    sc[2] = spread_core(2)
    arrive(aa[1])
    r1[1] = down_all(1)
    arrive(sc[2])
    aa[2] = gate_up(2, between_2)
    arrive(aa[2])
    r1[2] = down_all(2)
    arrive(sc[3])
    aa[3] = gate_up(3, between_3)
    arrive(aa[3])
    r1[3] = down_all(3)
    r2[2] = reduce_1(2, r1[2])
    r3[1] = reduce_2(1, r2[1])
    finish(0, r3[0])
    r2[3] = reduce_1(3, r1[3])
    r3[2] = reduce_2(2, r2[2])
    finish(1, r3[1])
    r3[3] = reduce_2(3, r2[3])
    finish(2, r3[2])
    finish(3, r3[3])
    for copy in sent:
        copy.wait_send()


def dense(tokens, expert_ids, gate_weights, gate_proj, up_proj, down_proj):
    tok_rows, half = tokens.shape
    experts_all = lax.axis_size("expert")
    hid, width = gate_proj.shape[1:]
    chunks = tok_rows // ROWS
    wide = (half - THIRD) // 2
    rows = experts_all * ROWS
    bf16, f32 = jnp.bfloat16, jnp.float32
    vmem = pl.BlockSpec(memory_space=pltpu.VMEM)
    hbm = pl.BlockSpec(memory_space=pl.ANY)
    copies = chunks * 30 + 11
    return pl.pallas_call(
        dense_kernel,
        out_shape=jax.ShapeDtypeStruct((tok_rows, half), bf16),
        in_specs=[vmem, vmem, vmem, hbm, hbm, hbm],
        out_specs=vmem,
        scratch_shapes=[
            pltpu.VMEM((chunks * 4, NZ, NY, NX, ROWS, wide), bf16),
            pltpu.VMEM((chunks * 2, NZ, NY, NX, ROWS, THIRD), bf16),
            pltpu.VMEM((NZ, NY, NX, experts_all, 128), f32),
            pltpu.VMEM((chunks, rows, 128), f32),
            pltpu.VMEM((hid, width), bf16),
            pltpu.VMEM((hid, width), bf16),
            pltpu.VMEM((2 * hid, half), bf16),
            pltpu.VMEM((chunks * 2, rows, hid), bf16),
            pltpu.VMEM((chunks * 2, NZ, NY, NX, ROWS, wide), bf16),
            pltpu.VMEM((chunks, NZ, NY, NX, ROWS, THIRD), bf16),
            pltpu.VMEM((chunks * 2, NZ, 2, ROWS, wide), bf16),
            pltpu.VMEM((chunks * 2, NZ, ROWS, wide), bf16),
            pltpu.VMEM((chunks, NZ - 1, 2, ROWS, wide), bf16),
            pltpu.VMEM((chunks, NZ - 1, NY, NX, ROWS, THIRD), bf16),
            pltpu.VMEM((chunks, NX, ROWS, THIRD), bf16),
            pltpu.VMEM((chunks, ROWS, THIRD), bf16),
            pltpu.SemaphoreType.DMA((3,)),
            pltpu.SemaphoreType.DMA((copies,)),
            pltpu.SemaphoreType.DMA((copies,)),
        ],
        compiler_params=pltpu.CompilerParams(
            collective_id=0, has_side_effects=True, vmem_limit_bytes=60 * 1024 * 1024
        ),
    )(tokens, expert_ids, gate_weights, gate_proj[0], up_proj[0], down_proj[0])


def solution(mesh):
    in_specs = (
        P("expert", "hidden"),
        P("expert", None),
        P("expert", None),
        P("expert", "hidden", None),
        P("expert", "hidden", None),
        P("expert", None, "hidden"),
    )
    out_specs = P("expert", "hidden")
    whole_blocks = mesh.shape["expert"] == NZ * NY * NX and mesh.shape["hidden"] == 2
    return jax.shard_map(
        dense if whole_blocks else routed,
        mesh=mesh, in_specs=in_specs, out_specs=out_specs, check_vma=False,
    )
```

```python
import functools

import jax
import jax.numpy as jnp
from jax import lax
from jax.experimental import pallas as pl
from jax.experimental.pallas import tpu as pltpu
from jax.sharding import PartitionSpec as P

MESH = pl.DeviceIdType.MESH
NZ, NY, NX = 4, 2, 2
ROWS = 16
TILE = 256
THIRD = 256


def routed(tokens, expert_ids, gate_weights, gate_proj, up_proj, down_proj):
    local_count = gate_proj.shape[0]
    experts_all = local_count * lax.axis_size("expert")
    tok_rows = tokens.shape[0]
    top_count = expert_ids.shape[1]
    capacity = 2 * tok_rows * top_count // experts_all
    flat_ids = expert_ids.reshape(-1)
    onehot = (flat_ids[:, None] == jnp.arange(experts_all, dtype=jnp.int32)[None, :]).astype(
        jnp.int32
    )
    slot_index = jnp.sum((jnp.cumsum(onehot, axis=0) - onehot) * onehot, axis=1)
    position = flat_ids * capacity + slot_index
    token_of = jnp.arange(tok_rows * top_count, dtype=jnp.int32) // top_count
    full_rows = lax.all_gather(tokens, "hidden", axis=1, tiled=True)
    packed = jnp.zeros((experts_all * capacity, full_rows.shape[1]), full_rows.dtype)
    packed = packed.at[position].set(full_rows[token_of])
    arrived = lax.all_to_all(
        packed.reshape(experts_all, capacity, full_rows.shape[1]),
        "expert",
        split_axis=0,
        concat_axis=1,
        tiled=True,
    )
    gate_sum = jnp.einsum("lrd,lfd->lfr", arrived, gate_proj, preferred_element_type=jnp.float32)
    up_sum = jnp.einsum("lrd,lfd->lfr", arrived, up_proj, preferred_element_type=jnp.float32)
    activation = (jax.nn.silu(gate_sum) * up_sum).astype(jnp.bfloat16)
    expert_out = jnp.einsum(
        "lfr,lfd->lrd",
        lax.all_gather(activation, "hidden", axis=1, tiled=True),
        down_proj,
        preferred_element_type=jnp.float32,
    ).astype(jnp.bfloat16)
    returned = lax.all_to_all(expert_out, "expert", split_axis=1, concat_axis=0, tiled=True)
    gathered = returned.reshape(experts_all * capacity, returned.shape[2])[position]
    gathered = gathered.reshape(tok_rows, top_count, returned.shape[2]).astype(jnp.float32)
    mixed = jnp.sum(gathered * gate_weights[:, :, None], axis=1)
    return mixed.astype(jnp.bfloat16)


def dense_kernel(
    tok_ref, wmat_ref, gate_hbm, up_hbm, down_hbm, out_ref,
    x_buf, xa_buf, w_buf, w_col, gate, up, down, act,
    part, parta, red1, red2, red3, reda1, reda2, reda3,
    local_sem, send_sem, recv_sem,
):
    chunks = tok_ref.shape[0] // ROWS
    wide = x_buf.shape[-1]
    half = tok_ref.shape[1]
    rows = NZ * NY * NX * ROWS
    hid = gate.shape[0]
    f32, bf16 = jnp.float32, jnp.bfloat16
    me = lax.axis_index("expert")
    core = lax.axis_index("hidden")
    z, y, x = me // (NY * NX), (me // NX) % NY, me % NX

    def at(zz, yy, xx):
        return ((zz * NY + yy) * NX + xx, core)

    x_peer, y_peer, sibling = at(z, y, 1 - x), at(z, 1 - y, x), (me, 1 - core)
    z_of = [lax.rem(z + d, NZ) for d in range(NZ)]
    z_peers = [at(z_of[d], y, x) for d in range(NZ)]

    loads = [
        pltpu.make_async_copy(src, dst, local_sem.at[i])
        for i, (src, dst) in enumerate(((gate_hbm, gate), (up_hbm, up), (down_hbm, down)))
    ]
    for load in loads:
        load.start()

    barrier = pltpu.get_barrier_semaphore()
    peers = [x_peer, y_peer, sibling] + z_peers[1:]
    for peer in peers:
        pl.semaphore_signal(barrier, inc=1, device_id=peer, device_id_type=MESH)
    for c in range(chunks):
        for p in range(2):
            x_buf[(c * 2 + core) * 2 + p, z, y, x] = tok_ref[
                c * ROWS : (c + 1) * ROWS, p * wide : (p + 1) * wide
            ]
        xa_buf[c * 2 + core, z, y, x] = tok_ref[c * ROWS : (c + 1) * ROWS, 2 * wide :]
    blank = jnp.zeros((wmat_ref.shape[0], 128 - wmat_ref.shape[1]), f32)
    w_buf[z, y, x] = jnp.concatenate([wmat_ref[...], blank], axis=1)
    pl.semaphore_wait(barrier, len(peers))

    sent = []

    def send(src, dst, peer):
        k = len(sent)
        copy = pltpu.make_async_remote_copy(
            src_ref=src, dst_ref=dst, send_sem=send_sem.at[k], recv_sem=recv_sem.at[k],
            device_id=peer, device_id_type=MESH,
        )
        copy.start()
        sent.append(copy)
        return copy

    def arrive(copies):
        for copy in copies:
            copy.wait_recv()

    def move(ref, peer):
        return send(ref, ref, peer)

    def spread_z(c):
        own = x_buf.at[pl.ds((c * 2 + core) * 2, 2), z, y, x]
        return [move(own, z_peers[d]) for d in range(1, NZ)] + [
            move(xa_buf.at[c * 2 + core, z, y, x], x_peer)
        ]

    def spread_1(c):
        i = (c * 2 + core) * 2
        return [
            move(x_buf.at[i, :, y, x], x_peer),
            move(x_buf.at[i + 1, :, y, x], y_peer),
            move(xa_buf.at[c * 2 + core, z, y], y_peer),
        ]

    def spread_2(c):
        i = (c * 2 + core) * 2
        third = xa_buf.at[c * 2 + core, z]
        return [
            move(x_buf.at[i, :, y], y_peer),
            move(x_buf.at[i + 1, :, :, x], x_peer),
        ] + [move(third, z_peers[d]) for d in range(1, NZ)]

    def spread_core(c):
        return [
            move(x_buf.at[pl.ds((c * 2 + core) * 2, 2)], sibling),
            move(xa_buf.at[c * 2 + core], sibling),
        ]

    def gate_up(c):
        def step(n, carry):
            cols = pl.ds(pl.multiple_of(n * TILE, TILE), TILE)
            sums = []
            for weight in (gate, up):
                total = None
                for k in range(6):
                    hh, p = k // 3, k % 3
                    if p < 2:
                        piece = x_buf[c * 4 + hh * 2 + p].reshape(rows, wide)
                    else:
                        piece = xa_buf[c * 2 + hh].reshape(rows, THIRD)
                    low = hh * half + p * wide
                    term = lax.dot_general(
                        piece,
                        weight[cols, low : low + piece.shape[1]],
                        (((1,), (1,)), ((), ())),
                        preferred_element_type=f32,
                    )
                    total = term if total is None else total + term
                sums.append(total)
            g, u = sums
            act[c * 2 + core, :, cols] = ((g / (1.0 + jnp.exp(-g))) * u).astype(bf16)
            return carry

        lax.fori_loop(0, hid // TILE, step, 0)
        return [move(act.at[c * 2 + core], sibling)]

    def down_tile(c, start, size):
        total = None
        for k in range(2):
            term = jnp.dot(
                act[c * 2 + k], down[k * hid : (k + 1) * hid, pl.ds(start, size)],
                preferred_element_type=f32,
            )
            total = term if total is None else total + term
        scale = w_col[c]
        total = total * jnp.concatenate([scale] * (size // 128), axis=1)
        return total.astype(bf16).reshape(NZ, NY, NX, ROWS, size)

    def down_part(c, p):
        def step(n, carry):
            into = pl.ds(pl.multiple_of(n * TILE, TILE), TILE)
            start = pl.multiple_of(p * wide + n * TILE, 128)
            part[c * 2 + p, :, :, :, :, into] = down_tile(c, start, TILE)
            return carry

        lax.fori_loop(0, wide // TILE, step, 0)
        rest = wide % TILE
        if rest:
            part[c * 2 + p, :, :, :, :, wide - rest :] = down_tile(c, (p + 1) * wide - rest, rest)

    def down_all(c):
        down_part(c, 0)
        down_part(c, 1)
        parta[c] = down_tile(c, 2 * wide, THIRD)

    def reduce_0(c):
        return [
            send(part.at[c * 2, :, 1 - y], red1.at[c * 2], y_peer),
            send(part.at[c * 2 + 1, :, :, 1 - x], red1.at[c * 2 + 1], x_peer),
        ] + [
            send(parta.at[c, z_of[d]], reda1.at[c, d - 1], z_peers[d]) for d in range(1, NZ)
        ]

    def reduce_1(c, copies):
        copies[0].wait_recv()
        for zz in range(NZ):
            red1[c * 2, zz] = (
                red1[c * 2, zz].astype(f32) + part[c * 2, zz, y].astype(f32)
            ).astype(bf16)
        first = send(red1.at[c * 2, :, 1 - x], red2.at[c * 2], x_peer)
        copies[1].wait_recv()
        for zz in range(NZ):
            for yy in range(NY):
                red1[c * 2 + 1, zz, yy] = (
                    red1[c * 2 + 1, zz, yy].astype(f32) + part[c * 2 + 1, zz, yy, x].astype(f32)
                ).astype(bf16)
        second = send(red1.at[c * 2 + 1, :, 1 - y], red2.at[c * 2 + 1], y_peer)
        arrive(copies[2:])
        total = parta[c, z].astype(f32)
        for d in range(NZ - 1):
            total = total + reda1[c, d].astype(f32)
        parta[c, z] = total.astype(bf16)
        return [first, second, send(parta.at[c, z, 1 - y], reda2.at[c], y_peer)]

    def reduce_2(c, copies):
        for p, (copy, mine) in enumerate(zip(copies, (x, y))):
            copy.wait_recv()
            for zz in range(NZ):
                red2[c * 2 + p, zz] = (
                    red2[c * 2 + p, zz].astype(f32) + red1[c * 2 + p, zz, mine].astype(f32)
                ).astype(bf16)
        out = [
            send(red2.at[pl.ds(c * 2, 2), z_of[d]], red3.at[c, d - 1], z_peers[d])
            for d in range(1, NZ)
        ]
        copies[2].wait_recv()
        reda2[c] = (reda2[c].astype(f32) + parta[c, z, y].astype(f32)).astype(bf16)
        return out + [send(reda2.at[c, 1 - x], reda3.at[c], x_peer)]

    def finish(c, copies):
        arrive(copies)
        for p in range(2):
            total = red2[c * 2 + p, z].astype(f32)
            for d in range(NZ - 1):
                total = total + red3[c, d, p].astype(f32)
            out_ref[c * ROWS : (c + 1) * ROWS, p * wide : (p + 1) * wide] = total.astype(bf16)
        total = reda2[c, x].astype(f32) + reda3[c].astype(f32)
        out_ref[c * ROWS : (c + 1) * ROWS, 2 * wide :] = total.astype(bf16)

    def columns_of_weights():
        lane = lax.broadcasted_iota(jnp.int32, w_buf.shape[3:], 0)
        picked = [
            jnp.sum(jnp.where(lane == me, w_buf[zz, yy, xx], 0.0), axis=0, keepdims=True)
            for zz in range(NZ) for yy in range(NY) for xx in range(NX)
        ]
        square = jnp.concatenate(picked + [jnp.zeros((128 - len(picked), 128), f32)], axis=0)
        turned = square.T
        for c in range(chunks):
            for b in range(len(picked)):
                w_col[c, b * ROWS : (b + 1) * ROWS, :] = jnp.broadcast_to(
                    turned[c * ROWS : (c + 1) * ROWS, b : b + 1], (ROWS, 128)
                )

    za = [None] * chunks
    s1, s2, sc = [None] * chunks, [None] * chunks, [None] * chunks
    aa, r1, r2, r3 = [None] * chunks, [None] * chunks, [None] * chunks, [None] * chunks

    za[0] = spread_z(0)
    wz = [move(w_buf.at[z, y, x], z_peers[d]) for d in range(1, NZ)]
    za[1] = spread_z(1)
    arrive(za[0])
    s1[0] = spread_1(0)
    arrive(wz)
    wx = [move(w_buf.at[:, y, x], x_peer)]
    za[2] = spread_z(2)
    arrive(s1[0])
    s2[0] = spread_2(0)
    arrive(wx)
    wy = [move(w_buf.at[:, y], y_peer)]
    arrive(za[1])
    s1[1] = spread_1(1)
    za[3] = spread_z(3)
    arrive(s1[1])
    s2[1] = spread_2(1)
    arrive(wy)
    columns_of_weights()
    arrive(s2[0])
    sc[0] = spread_core(0)
    arrive(za[2])
    s1[2] = spread_1(2)
    loads[0].wait()
    loads[1].wait()
    loads[2].wait()
    arrive(sc[0])
    aa[0] = gate_up(0)
    arrive(s1[2])
    s2[2] = spread_2(2)
    arrive(s2[1])
    sc[1] = spread_core(1)
    arrive(za[3])
    s1[3] = spread_1(3)
    arrive(sc[1])
    aa[1] = gate_up(1)
    arrive(s1[3])
    s2[3] = spread_2(3)
    arrive(aa[0])
    down_all(0)
    r1[0] = reduce_0(0)
    arrive(s2[2])
    sc[2] = spread_core(2)
    arrive(aa[1])
    down_all(1)
    arrive(sc[2])
    aa[2] = gate_up(2)
    arrive(s2[3])
    sc[3] = spread_core(3)
    r1[1] = reduce_0(1)
    arrive(aa[2])
    down_all(2)
    r1[2] = reduce_0(2)
    r2[0] = reduce_1(0, r1[0])
    arrive(sc[3])
    aa[3] = gate_up(3)
    r2[1] = reduce_1(1, r1[1])
    r3[0] = reduce_2(0, r2[0])
    arrive(aa[3])
    down_all(3)
    r1[3] = reduce_0(3)
    r2[2] = reduce_1(2, r1[2])
    r3[1] = reduce_2(1, r2[1])
    finish(0, r3[0])
    r2[3] = reduce_1(3, r1[3])
    r3[2] = reduce_2(2, r2[2])
    finish(1, r3[1])
    r3[3] = reduce_2(3, r2[3])
    finish(2, r3[2])
    finish(3, r3[3])
    for copy in sent:
        copy.wait_send()


def dense(tokens, expert_ids, gate_weights, gate_proj, up_proj, down_proj):
    tok_rows, half = tokens.shape
    experts_all = lax.axis_size("expert")
    hid, width = gate_proj.shape[1:]
    chunks = tok_rows // ROWS
    wide = (half - THIRD) // 2
    rows = experts_all * ROWS
    chosen = expert_ids[None, :, :] == jnp.arange(experts_all, dtype=jnp.int32)[:, None, None]
    wmat = jnp.sum(jnp.where(chosen, gate_weights[None], 0.0), axis=2)
    bf16, f32 = jnp.bfloat16, jnp.float32
    vmem = pl.BlockSpec(memory_space=pltpu.VMEM)
    hbm = pl.BlockSpec(memory_space=pl.ANY)
    copies = chunks * 27 + 5
    return pl.pallas_call(
        dense_kernel,
        out_shape=jax.ShapeDtypeStruct((tok_rows, half), bf16),
        in_specs=[vmem, vmem, hbm, hbm, hbm],
        out_specs=vmem,
        scratch_shapes=[
            pltpu.VMEM((chunks * 4, NZ, NY, NX, ROWS, wide), bf16),
            pltpu.VMEM((chunks * 2, NZ, NY, NX, ROWS, THIRD), bf16),
            pltpu.VMEM((NZ, NY, NX, experts_all, 128), f32),
            pltpu.VMEM((chunks, rows, 128), f32),
            pltpu.VMEM((hid, width), bf16),
            pltpu.VMEM((hid, width), bf16),
            pltpu.VMEM((2 * hid, half), bf16),
            pltpu.VMEM((chunks * 2, rows, hid), bf16),
            pltpu.VMEM((chunks * 2, NZ, NY, NX, ROWS, wide), bf16),
            pltpu.VMEM((chunks, NZ, NY, NX, ROWS, THIRD), bf16),
            pltpu.VMEM((chunks * 2, NZ, 2, ROWS, wide), bf16),
            pltpu.VMEM((chunks * 2, NZ, ROWS, wide), bf16),
            pltpu.VMEM((chunks, NZ - 1, 2, ROWS, wide), bf16),
            pltpu.VMEM((chunks, NZ - 1, NY, NX, ROWS, THIRD), bf16),
            pltpu.VMEM((chunks, NX, ROWS, THIRD), bf16),
            pltpu.VMEM((chunks, ROWS, THIRD), bf16),
            pltpu.SemaphoreType.DMA((3,)),
            pltpu.SemaphoreType.DMA((copies,)),
            pltpu.SemaphoreType.DMA((copies,)),
        ],
        compiler_params=pltpu.CompilerParams(
            collective_id=0, has_side_effects=True, vmem_limit_bytes=60 * 1024 * 1024
        ),
    )(tokens, wmat, gate_proj[0], up_proj[0], down_proj[0])


def solution(mesh):
    in_specs = (
        P("expert", "hidden"),
        P("expert", None),
        P("expert", None),
        P("expert", "hidden", None),
        P("expert", "hidden", None),
        P("expert", None, "hidden"),
    )
    out_specs = P("expert", "hidden")
    whole_blocks = mesh.shape["expert"] == NZ * NY * NX and mesh.shape["hidden"] == 2
    return jax.shard_map(
        dense if whole_blocks else routed,
        mesh=mesh, in_specs=in_specs, out_specs=out_specs, check_vma=False,
    )
```

```python
import functools

import jax
import jax.numpy as jnp
from jax import lax
from jax.experimental import pallas as pl
from jax.experimental.pallas import tpu as pltpu
from jax.sharding import PartitionSpec as P

MESH = pl.DeviceIdType.MESH
NZ, NY, NX = 4, 2, 2
ROWS = 16
TILE = 256
THIRD = 256


def routed(tokens, expert_ids, gate_weights, gate_proj, up_proj, down_proj):
    local_count = gate_proj.shape[0]
    experts_all = local_count * lax.axis_size("expert")
    tok_rows = tokens.shape[0]
    top_count = expert_ids.shape[1]
    capacity = 2 * tok_rows * top_count // experts_all
    flat_ids = expert_ids.reshape(-1)
    onehot = (flat_ids[:, None] == jnp.arange(experts_all, dtype=jnp.int32)[None, :]).astype(
        jnp.int32
    )
    slot_index = jnp.sum((jnp.cumsum(onehot, axis=0) - onehot) * onehot, axis=1)
    position = flat_ids * capacity + slot_index
    token_of = jnp.arange(tok_rows * top_count, dtype=jnp.int32) // top_count
    full_rows = lax.all_gather(tokens, "hidden", axis=1, tiled=True)
    packed = jnp.zeros((experts_all * capacity, full_rows.shape[1]), full_rows.dtype)
    packed = packed.at[position].set(full_rows[token_of])
    arrived = lax.all_to_all(
        packed.reshape(experts_all, capacity, full_rows.shape[1]),
        "expert",
        split_axis=0,
        concat_axis=1,
        tiled=True,
    )
    gate_sum = jnp.einsum("lrd,lfd->lfr", arrived, gate_proj, preferred_element_type=jnp.float32)
    up_sum = jnp.einsum("lrd,lfd->lfr", arrived, up_proj, preferred_element_type=jnp.float32)
    activation = (jax.nn.silu(gate_sum) * up_sum).astype(jnp.bfloat16)
    expert_out = jnp.einsum(
        "lfr,lfd->lrd",
        lax.all_gather(activation, "hidden", axis=1, tiled=True),
        down_proj,
        preferred_element_type=jnp.float32,
    ).astype(jnp.bfloat16)
    returned = lax.all_to_all(expert_out, "expert", split_axis=1, concat_axis=0, tiled=True)
    gathered = returned.reshape(experts_all * capacity, returned.shape[2])[position]
    gathered = gathered.reshape(tok_rows, top_count, returned.shape[2]).astype(jnp.float32)
    mixed = jnp.sum(gathered * gate_weights[:, :, None], axis=1)
    return mixed.astype(jnp.bfloat16)


def dense_kernel(
    tok_ref, wmat_ref, gate_hbm, up_hbm, down_hbm, out_ref,
    x_buf, xa_buf, w_buf, w_col, gate, up, down, act,
    part, parta, red1, red2, red3, reda1, reda2, reda3,
    local_sem, send_sem, recv_sem,
):
    chunks = tok_ref.shape[0] // ROWS
    wide = x_buf.shape[-1]
    half = tok_ref.shape[1]
    rows = NZ * NY * NX * ROWS
    hid = gate.shape[0]
    f32, bf16 = jnp.float32, jnp.bfloat16
    me = lax.axis_index("expert")
    core = lax.axis_index("hidden")
    z, y, x = me // (NY * NX), (me // NX) % NY, me % NX

    def at(zz, yy, xx):
        return ((zz * NY + yy) * NX + xx, core)

    x_peer, y_peer, sibling = at(z, y, 1 - x), at(z, 1 - y, x), (me, 1 - core)
    z_of = [lax.rem(z + d, NZ) for d in range(NZ)]
    z_peers = [at(z_of[d], y, x) for d in range(NZ)]

    loads = [
        pltpu.make_async_copy(src, dst, local_sem.at[i])
        for i, (src, dst) in enumerate(((gate_hbm, gate), (up_hbm, up), (down_hbm, down)))
    ]
    for load in loads:
        load.start()

    barrier = pltpu.get_barrier_semaphore()
    peers = [x_peer, y_peer, sibling] + z_peers[1:]
    for peer in peers:
        pl.semaphore_signal(barrier, inc=1, device_id=peer, device_id_type=MESH)
    for c in range(chunks):
        for p in range(2):
            x_buf[(c * 2 + core) * 2 + p, z, y, x] = tok_ref[
                c * ROWS : (c + 1) * ROWS, p * wide : (p + 1) * wide
            ]
        xa_buf[c * 2 + core, z, y, x] = tok_ref[c * ROWS : (c + 1) * ROWS, 2 * wide :]
    blank = jnp.zeros((wmat_ref.shape[0], 128 - wmat_ref.shape[1]), f32)
    w_buf[z, y, x] = jnp.concatenate([wmat_ref[...], blank], axis=1)
    pl.semaphore_wait(barrier, len(peers))

    sent = []

    def send(src, dst, peer):
        k = len(sent)
        copy = pltpu.make_async_remote_copy(
            src_ref=src, dst_ref=dst, send_sem=send_sem.at[k], recv_sem=recv_sem.at[k],
            device_id=peer, device_id_type=MESH,
        )
        copy.start()
        sent.append(copy)
        return copy

    def arrive(copies):
        for copy in copies:
            copy.wait_recv()

    def move(ref, peer):
        return send(ref, ref, peer)

    def spread_z(c):
        own = x_buf.at[pl.ds((c * 2 + core) * 2, 2), z, y, x]
        return [move(own, z_peers[d]) for d in range(1, NZ)] + [
            move(xa_buf.at[c * 2 + core, z, y, x], x_peer)
        ]

    def spread_1(c):
        i = (c * 2 + core) * 2
        return [
            move(x_buf.at[i, :, y, x], x_peer),
            move(x_buf.at[i + 1, :, y, x], y_peer),
            move(xa_buf.at[c * 2 + core, z, y], y_peer),
        ]

    def spread_1_first(c, copies):
        i = (c * 2 + core) * 2

        def pair(zz):
            return [
                move(x_buf.at[i, zz, y, x], x_peer),
                move(x_buf.at[i + 1, zz, y, x], y_peer),
            ]

        out = pair(z)
        for d in range(1, NZ):
            copies[d - 1].wait_recv()
            out = out + pair(z_of[NZ - d])
        copies[NZ - 1].wait_recv()
        return out + [move(xa_buf.at[c * 2 + core, z, y], y_peer)]

    def spread_2(c):
        i = (c * 2 + core) * 2
        third = xa_buf.at[c * 2 + core, z]
        return [
            move(x_buf.at[i, :, y], y_peer),
            move(x_buf.at[i + 1, :, :, x], x_peer),
        ] + [move(third, z_peers[d]) for d in range(1, NZ)]

    def spread_core(c):
        return [
            move(x_buf.at[pl.ds((c * 2 + core) * 2, 2)], sibling),
            move(xa_buf.at[c * 2 + core], sibling),
        ]

    def gate_up(c):
        def step(n, carry):
            cols = pl.ds(pl.multiple_of(n * TILE, TILE), TILE)
            sums = []
            for weight in (gate, up):
                total = None
                for k in range(6):
                    hh, p = k // 3, k % 3
                    if p < 2:
                        piece = x_buf[c * 4 + hh * 2 + p].reshape(rows, wide)
                    else:
                        piece = xa_buf[c * 2 + hh].reshape(rows, THIRD)
                    low = hh * half + p * wide
                    term = lax.dot_general(
                        piece,
                        weight[cols, low : low + piece.shape[1]],
                        (((1,), (1,)), ((), ())),
                        preferred_element_type=f32,
                    )
                    total = term if total is None else total + term
                sums.append(total)
            g, u = sums
            act[c * 2 + core, :, cols] = ((g / (1.0 + jnp.exp(-g))) * u).astype(bf16)
            return carry

        lax.fori_loop(0, hid // TILE, step, 0)
        return [move(act.at[c * 2 + core], sibling)]

    def down_tile(c, start, size):
        total = None
        for k in range(2):
            term = jnp.dot(
                act[c * 2 + k], down[k * hid : (k + 1) * hid, pl.ds(start, size)],
                preferred_element_type=f32,
            )
            total = term if total is None else total + term
        scale = w_col[c]
        total = total * jnp.concatenate([scale] * (size // 128), axis=1)
        return total.astype(bf16).reshape(NZ, NY, NX, ROWS, size)

    def down_part(c, p):
        def step(n, carry):
            into = pl.ds(pl.multiple_of(n * TILE, TILE), TILE)
            start = pl.multiple_of(p * wide + n * TILE, 128)
            part[c * 2 + p, :, :, :, :, into] = down_tile(c, start, TILE)
            return carry

        lax.fori_loop(0, wide // TILE, step, 0)
        rest = wide % TILE
        if rest:
            part[c * 2 + p, :, :, :, :, wide - rest :] = down_tile(c, (p + 1) * wide - rest, rest)

    def down_all(c):
        down_part(c, 0)
        first = send(part.at[c * 2, :, 1 - y], red1.at[c * 2], y_peer)
        down_part(c, 1)
        second = send(part.at[c * 2 + 1, :, :, 1 - x], red1.at[c * 2 + 1], x_peer)
        parta[c] = down_tile(c, 2 * wide, THIRD)
        return [first, second] + [
            send(parta.at[c, z_of[d]], reda1.at[c, d - 1], z_peers[d]) for d in range(1, NZ)
        ]

    def reduce_1(c, copies):
        copies[0].wait_recv()
        for zz in range(NZ):
            red1[c * 2, zz] = (
                red1[c * 2, zz].astype(f32) + part[c * 2, zz, y].astype(f32)
            ).astype(bf16)
        first = send(red1.at[c * 2, :, 1 - x], red2.at[c * 2], x_peer)
        copies[1].wait_recv()
        for zz in range(NZ):
            for yy in range(NY):
                red1[c * 2 + 1, zz, yy] = (
                    red1[c * 2 + 1, zz, yy].astype(f32) + part[c * 2 + 1, zz, yy, x].astype(f32)
                ).astype(bf16)
        second = send(red1.at[c * 2 + 1, :, 1 - y], red2.at[c * 2 + 1], y_peer)
        arrive(copies[2:])
        total = parta[c, z].astype(f32)
        for d in range(NZ - 1):
            total = total + reda1[c, d].astype(f32)
        parta[c, z] = total.astype(bf16)
        return [first, second, send(parta.at[c, z, 1 - y], reda2.at[c], y_peer)]

    def reduce_2(c, copies):
        for p, (copy, mine) in enumerate(zip(copies, (x, y))):
            copy.wait_recv()
            for zz in range(NZ):
                red2[c * 2 + p, zz] = (
                    red2[c * 2 + p, zz].astype(f32) + red1[c * 2 + p, zz, mine].astype(f32)
                ).astype(bf16)
        out = [
            send(red2.at[pl.ds(c * 2, 2), z_of[d]], red3.at[c, d - 1], z_peers[d])
            for d in range(1, NZ)
        ]
        copies[2].wait_recv()
        reda2[c] = (reda2[c].astype(f32) + parta[c, z, y].astype(f32)).astype(bf16)
        return out + [send(reda2.at[c, 1 - x], reda3.at[c], x_peer)]

    def finish(c, copies):
        arrive(copies)
        for p in range(2):
            total = red2[c * 2 + p, z].astype(f32)
            for d in range(NZ - 1):
                total = total + red3[c, d, p].astype(f32)
            out_ref[c * ROWS : (c + 1) * ROWS, p * wide : (p + 1) * wide] = total.astype(bf16)
        total = reda2[c, x].astype(f32) + reda3[c].astype(f32)
        out_ref[c * ROWS : (c + 1) * ROWS, 2 * wide :] = total.astype(bf16)

    def columns_of_weights():
        lane = lax.broadcasted_iota(jnp.int32, w_buf.shape[3:], 0)
        picked = [
            jnp.sum(jnp.where(lane == me, w_buf[zz, yy, xx], 0.0), axis=0, keepdims=True)
            for zz in range(NZ) for yy in range(NY) for xx in range(NX)
        ]
        square = jnp.concatenate(picked + [jnp.zeros((128 - len(picked), 128), f32)], axis=0)
        turned = square.T
        for c in range(chunks):
            for b in range(len(picked)):
                w_col[c, b * ROWS : (b + 1) * ROWS, :] = jnp.broadcast_to(
                    turned[c * ROWS : (c + 1) * ROWS, b : b + 1], (ROWS, 128)
                )

    za = [None] * chunks
    s1, s2, sc = [None] * chunks, [None] * chunks, [None] * chunks
    aa, r1, r2, r3 = [None] * chunks, [None] * chunks, [None] * chunks, [None] * chunks

    za[0] = spread_z(0)
    wz = [move(w_buf.at[z, y, x], z_peers[d]) for d in range(1, NZ)]
    za[1] = spread_z(1)
    s1[0] = spread_1_first(0, za[0])
    arrive(wz)
    wx = [move(w_buf.at[:, y, x], x_peer)]
    za[2] = spread_z(2)
    arrive(s1[0])
    s2[0] = spread_2(0)
    arrive(wx)
    wy = [move(w_buf.at[:, y], y_peer)]
    arrive(za[1])
    s1[1] = spread_1(1)
    za[3] = spread_z(3)
    arrive(s1[1])
    s2[1] = spread_2(1)
    arrive(wy)
    columns_of_weights()
    arrive(s2[0])
    sc[0] = spread_core(0)
    arrive(za[2])
    s1[2] = spread_1(2)
    loads[0].wait()
    loads[1].wait()
    loads[2].wait()
    arrive(sc[0])
    aa[0] = gate_up(0)
    arrive(s1[2])
    s2[2] = spread_2(2)
    arrive(s2[1])
    sc[1] = spread_core(1)
    arrive(za[3])
    s1[3] = spread_1(3)
    arrive(sc[1])
    aa[1] = gate_up(1)
    arrive(s1[3])
    s2[3] = spread_2(3)
    arrive(aa[0])
    r1[0] = down_all(0)
    arrive(s2[2])
    sc[2] = spread_core(2)
    arrive(aa[1])
    r1[1] = down_all(1)
    arrive(sc[2])
    aa[2] = gate_up(2)
    r2[0] = reduce_1(0, r1[0])
    arrive(s2[3])
    sc[3] = spread_core(3)
    arrive(aa[2])
    r1[2] = down_all(2)
    arrive(sc[3])
    aa[3] = gate_up(3)
    r2[1] = reduce_1(1, r1[1])
    r3[0] = reduce_2(0, r2[0])
    arrive(aa[3])
    r1[3] = down_all(3)
    r2[2] = reduce_1(2, r1[2])
    r3[1] = reduce_2(1, r2[1])
    finish(0, r3[0])
    r2[3] = reduce_1(3, r1[3])
    r3[2] = reduce_2(2, r2[2])
    finish(1, r3[1])
    r3[3] = reduce_2(3, r2[3])
    finish(2, r3[2])
    finish(3, r3[3])
    for copy in sent:
        copy.wait_send()


def dense(tokens, expert_ids, gate_weights, gate_proj, up_proj, down_proj):
    tok_rows, half = tokens.shape
    experts_all = lax.axis_size("expert")
    hid, width = gate_proj.shape[1:]
    chunks = tok_rows // ROWS
    wide = (half - THIRD) // 2
    rows = experts_all * ROWS
    chosen = expert_ids[None, :, :] == jnp.arange(experts_all, dtype=jnp.int32)[:, None, None]
    wmat = jnp.sum(jnp.where(chosen, gate_weights[None], 0.0), axis=2)
    bf16, f32 = jnp.bfloat16, jnp.float32
    vmem = pl.BlockSpec(memory_space=pltpu.VMEM)
    hbm = pl.BlockSpec(memory_space=pl.ANY)
    copies = chunks * 27 + 11
    return pl.pallas_call(
        dense_kernel,
        out_shape=jax.ShapeDtypeStruct((tok_rows, half), bf16),
        in_specs=[vmem, vmem, hbm, hbm, hbm],
        out_specs=vmem,
        scratch_shapes=[
            pltpu.VMEM((chunks * 4, NZ, NY, NX, ROWS, wide), bf16),
            pltpu.VMEM((chunks * 2, NZ, NY, NX, ROWS, THIRD), bf16),
            pltpu.VMEM((NZ, NY, NX, experts_all, 128), f32),
            pltpu.VMEM((chunks, rows, 128), f32),
            pltpu.VMEM((hid, width), bf16),
            pltpu.VMEM((hid, width), bf16),
            pltpu.VMEM((2 * hid, half), bf16),
            pltpu.VMEM((chunks * 2, rows, hid), bf16),
            pltpu.VMEM((chunks * 2, NZ, NY, NX, ROWS, wide), bf16),
            pltpu.VMEM((chunks, NZ, NY, NX, ROWS, THIRD), bf16),
            pltpu.VMEM((chunks * 2, NZ, 2, ROWS, wide), bf16),
            pltpu.VMEM((chunks * 2, NZ, ROWS, wide), bf16),
            pltpu.VMEM((chunks, NZ - 1, 2, ROWS, wide), bf16),
            pltpu.VMEM((chunks, NZ - 1, NY, NX, ROWS, THIRD), bf16),
            pltpu.VMEM((chunks, NX, ROWS, THIRD), bf16),
            pltpu.VMEM((chunks, ROWS, THIRD), bf16),
            pltpu.SemaphoreType.DMA((3,)),
            pltpu.SemaphoreType.DMA((copies,)),
            pltpu.SemaphoreType.DMA((copies,)),
        ],
        compiler_params=pltpu.CompilerParams(
            collective_id=0, has_side_effects=True, vmem_limit_bytes=60 * 1024 * 1024
        ),
    )(tokens, wmat, gate_proj[0], up_proj[0], down_proj[0])


def solution(mesh):
    in_specs = (
        P("expert", "hidden"),
        P("expert", None),
        P("expert", None),
        P("expert", "hidden", None),
        P("expert", "hidden", None),
        P("expert", None, "hidden"),
    )
    out_specs = P("expert", "hidden")
    whole_blocks = mesh.shape["expert"] == NZ * NY * NX and mesh.shape["hidden"] == 2
    return jax.shard_map(
        dense if whole_blocks else routed,
        mesh=mesh, in_specs=in_specs, out_specs=out_specs, check_vma=False,
    )
```
